32 devices in a mesh: groups: 2 (over y), leaf: 16 (over z, x, core).
Axes of the slice: x: 2, y: 2, z: 4, core: 2. Of those that a mesh axis runs over, the one named last changes fastest.
Arguments:
- points: float32 [32, 262144], P(None, ('groups', 'leaf')), parts along dimension 1, may hold values from -6 to 6
- solution: float32 [262144], P(('groups', 'leaf')), parts along dimension 0, may hold values from -6 to 6
- residual: float32 [262144], P(('groups', 'leaf')), parts along dimension 0
- direction: float32 [262144], P(('groups', 'leaf')), parts along dimension 0
- ridge_weight: float32 [2], P('groups'), parts along dimension 0, may hold values from 0.5 to 2
- kernel_rate: float32 [2], P('groups'), parts along dimension 0, may hold values from 0.0390625 to 0.0625
- tree_perm: int32 [32, 8192], P(('groups', 'leaf')), parts along dimension 0, may hold values from 0 to 8191, each once within a row
- local_skeleton: float32 [1984, 32, 256], P(('groups', 'leaf')), parts along dimension 0, may hold values from -6 to 6
- local_transfer: bfloat16 [1984, 256, 256], P(('groups', 'leaf')), parts along dimension 0, may hold values from -0.375 to 0.375
- cross_skeleton: float32 [128, 2, 32, 256], P(('groups', 'leaf')), parts along dimension 0, as said below
- cross_transfer: bfloat16 [96, 2, 256, 256], P(('groups', 'leaf')), parts along dimension 0, as said below
- near_target: int32 [8192], P(('groups', 'leaf')), parts along dimension 0, may hold values from 0 to 511, as said below
- near_source: int32 [8192], P(('groups', 'leaf')), parts along dimension 0, may hold values from 0 to 511, as said below
- tile_count: int32 [32], P(('groups', 'leaf')), parts along dimension 0, may hold values from 64 to 256, as said below
Outputs:
- new_solution: float32 [262144], P(('groups', 'leaf')), parts along dimension 0
- new_residual: float32 [262144], P(('groups', 'leaf')), parts along dimension 0
- new_direction: float32 [262144], P(('groups', 'leaf')), parts along dimension 0
The draws below stay inside these ranges and needn't reach their ends.
There are 2 independent parts, one for each index of `groups`. The reference program is written for one: setup_inputs(seed, part) draws one part's arguments, and reference() takes and returns one part's arrays. A program takes and returns all parts, laid end to end along the dimension named above; each array names one. Nothing has to cross between parts.
Inputs may be any that keep to these rules, and one draw needn't show every extreme that they name: `tree_perm`: each row is a permutation of the device's 8192 positions. `near_target`: slot s of device d is a leaf of device d; its first 32 slots name its leaves in order and pair them with themselves. A pair listed twice counts twice. `near_source`: A source lies at most 16 leaves from its target in tree order, within the leaves of the problem; every device has a live pair at distance exactly 16 on each side or mirrored at an end. `tile_count`: slots at or past a device's count are not part of the operator. `cross_skeleton`: entries for level l are equal on all devices with the same level l ancestor; member 1 equals member 0 of the devices of the sibling. `cross_transfer`: entries for level l are equal on all devices with the same level l ancestor; member 1 equals member 0 of the devices of the sibling.
All inputs are finite; a program needn't handle non-finite values.
Results may differ from the reference program's by a relative error of at most 0.0003.
Values sent between devices are 32-bit elements; how exact they have to be, the bound alone decides.
A program may use at most 128 MiB of HBM per device.

```python
import math
import jax
import jax.numpy as jnp
from jax import lax

DIM = 32
RANK = 256
LEAF = 256
LEAVES_DEV = 32
LEVELS_X = 4
LOCAL_NODES = 62
REACH = 16
TILE_CAP = 256
POINTS_DEV = 8192
LEAVES = 512
POINTS = 131072
N_LEAF = 16


def ramp_vector(key, top_scale):
    key_one = jax.random.fold_in(key, 0)
    key_three = jax.random.fold_in(key, 2)
    normal_part = jnp.clip(jax.random.normal(key_one, (POINTS,), jnp.float32), -6.0, 6.0)
    mixed = normal_part
    block_scale = jnp.exp(jax.random.uniform(key_three, (POINTS // LEAF,), jnp.float32, jnp.log(0.3), jnp.log(3.0)))
    ramp = 1.0 + (top_scale - 1.0) * jnp.arange(POINTS, dtype=jnp.float32) / POINTS
    return mixed * jnp.repeat(block_scale, LEAF) * ramp


def draw_residual(key, part):
    key = jax.random.fold_in(key, 11)
    return ramp_vector(key, 3.0)


def draw_direction(key, part):
    key = jax.random.fold_in(key, 12)
    return ramp_vector(key, 3.0)


def draw_cross_skeleton(key, part):
    key = jax.random.fold_in(key, 21)
    device_ids = jnp.arange(N_LEAF, dtype=jnp.int32)
    layers = []
    for level in range(LEVELS_X):
        table = jax.random.normal(jax.random.fold_in(key, level), (N_LEAF >> level, DIM, RANK), jnp.float32)
        table = jnp.clip(table, -6.0, 6.0)
        owner = jnp.right_shift(device_ids, level)
        layers.append(jnp.stack([table[owner], table[jnp.bitwise_xor(owner, 1)]], axis=1))
    return jnp.stack(layers, axis=1).reshape(N_LEAF * LEVELS_X, 2, DIM, RANK)


def draw_cross_transfer(key, part):
    key = jax.random.fold_in(key, 22)
    device_ids = jnp.arange(N_LEAF, dtype=jnp.int32)
    layers = []
    for level in range(LEVELS_X - 1):
        table = jax.random.normal(jax.random.fold_in(key, level), (N_LEAF >> level, RANK, RANK), jnp.float32)
        table = (jnp.clip(table, -6.0, 6.0) * RANK ** (-0.5)).astype(jnp.bfloat16)
        owner = jnp.right_shift(device_ids, level)
        layers.append(jnp.stack([table[owner], table[jnp.bitwise_xor(owner, 1)]], axis=1))
    return jnp.stack(layers, axis=1).reshape(N_LEAF * (LEVELS_X - 1), 2, RANK, RANK)


def tile_pairs(key):
    key_one, key_two, key_three = jax.random.split(jax.random.fold_in(key, 31), 3)
    device_ids = jnp.arange(N_LEAF, dtype=jnp.int32)[:, None]
    slot_ids = jnp.arange(TILE_CAP, dtype=jnp.int32)[None, :]
    local_leaf = jax.random.randint(key_one, (N_LEAF, TILE_CAP), 0, LEAVES_DEV, jnp.int32)
    local_leaf = jnp.where(slot_ids < LEAVES_DEV, slot_ids, local_leaf)
    distance = jax.random.randint(key_two, (N_LEAF, TILE_CAP), 1, REACH + 1, jnp.int32)
    direction_sign = jax.random.randint(key_three, (N_LEAF, TILE_CAP), 0, 2, jnp.int32) * 2 - 1
    offset = distance * direction_sign
    offset = jnp.where(slot_ids == LEAVES_DEV, REACH, offset)
    offset = jnp.where(slot_ids == LEAVES_DEV + 1, -REACH, offset)
    offset = jnp.where(slot_ids < LEAVES_DEV, 0, offset)
    target = device_ids * LEAVES_DEV + local_leaf
    source = target + offset
    outside = jnp.logical_or(source < 0, source >= LEAVES)
    source = jnp.where(outside, target - offset, source)
    return (target.reshape(-1), source.reshape(-1))


def draw_near_target(key, part):
    return tile_pairs(key)[0]


def draw_near_source(key, part):
    return tile_pairs(key)[1]


def draw_tile_count(key, part):
    key = jax.random.fold_in(key, 41)
    key_one, key_two, key_three, key_four = jax.random.split(key, 4)
    counts = jax.random.randint(key_one, (N_LEAF,), TILE_CAP // 4, TILE_CAP // 2 + 1, jnp.int32)
    full_rows = jax.random.randint(key_two, (N_LEAF,), 0, 8, jnp.int32) == 0
    counts = jnp.where(full_rows, TILE_CAP, counts)
    first_pick = jax.random.randint(key_three, (), 0, N_LEAF, jnp.int32)
    second_pick = (first_pick + 1 + jax.random.randint(key_four, (), 0, N_LEAF - 1, jnp.int32)) % N_LEAF
    counts = counts.at[first_pick].set(TILE_CAP)
    counts = counts.at[second_pick].set(TILE_CAP // 4)
    return counts


def levels(own_key, extent, cuts, least, high):
    def one(dim, blocks):
        draws = jax.random.uniform(jax.random.fold_in(jax.random.fold_in(own_key, 6), dim), (blocks,), jnp.float32, least / len(cuts), high / len(cuts))
        return jnp.repeat(jnp.exp(draws), extent[dim] // blocks).reshape((-1,) + (1,) * (len(extent) - dim - 1))

    gain = one(*cuts[0])
    for cut in cuts[1:]:
        gain = gain * one(*cut)
    return gain


def bell_draw(key, extent, width, reach, cuts=(), held_as=jnp.bfloat16):
    drawn = width * jax.random.normal(key, extent, jnp.float32)
    if cuts:
        drawn = drawn * levels(key, extent, cuts, -0.22, 0.18)
    return jnp.clip(drawn, -reach, reach).astype(held_as)


def setup_inputs(seed: int = 0, part: int = 0) -> dict:
    key_list = jax.random.split(jax.random.key(seed), 15)
    part_keys = jax.random.split(jax.random.fold_in(key_list[14], part), 15)
    return {
        "points": bell_draw(part_keys[0], (DIM, POINTS), 1.0, 6.0, ((1, 16),), jnp.float32),
        "solution": bell_draw(part_keys[1], (POINTS,), 1.0, 6.0, ((0, 16),), jnp.float32),
        "residual": draw_residual(jax.random.fold_in(jax.random.fold_in(key_list[14], part), 71), part),
        "direction": draw_direction(jax.random.fold_in(jax.random.fold_in(key_list[14], part), 71), part),
        "ridge_weight": jnp.clip(jnp.exp(jax.random.uniform(part_keys[4], (1,), jnp.float32, math.log(0.5), math.log(2.0))), 0.5, 2.0),
        "kernel_rate": jnp.clip(jnp.exp(jax.random.uniform(part_keys[5], (1,), jnp.float32, math.log(0.0390625), math.log(0.0625))), 0.0390625, 0.0625),
        "tree_perm": jax.vmap(lambda own: jax.random.permutation(own, POINTS_DEV))(jax.random.split(part_keys[6], N_LEAF)).reshape((N_LEAF, POINTS_DEV)).astype(jnp.int32),
        "local_skeleton": bell_draw(part_keys[7], (N_LEAF * LOCAL_NODES, DIM, RANK), 1.0, 6.0, ((0, 16),), jnp.float32),
        "local_transfer": bell_draw(part_keys[8], (N_LEAF * LOCAL_NODES, RANK, RANK), RANK ** -0.5, 0.375, ((0, 16),)),
        "cross_skeleton": draw_cross_skeleton(jax.random.fold_in(jax.random.fold_in(key_list[14], part), 71), part),
        "cross_transfer": draw_cross_transfer(jax.random.fold_in(jax.random.fold_in(key_list[14], part), 71), part),
        "near_target": draw_near_target(jax.random.fold_in(jax.random.fold_in(key_list[14], part), 71), part),
        "near_source": draw_near_source(jax.random.fold_in(jax.random.fold_in(key_list[14], part), 71), part),
        "tile_count": draw_tile_count(jax.random.fold_in(jax.random.fold_in(key_list[14], part), 71), part),
    }


epsilon = 1e-6
half_root = 0.5 ** 0.5


def kernel_block(first_set, second_set, rate_value):
    first_norms = jnp.sum(first_set * first_set, axis=-2)
    second_norms = jnp.sum(second_set * second_set, axis=-2)
    inner_prod = jnp.einsum("...dm,...dn->...mn", first_set, second_set, precision=lax.Precision.HIGHEST)
    distance = first_norms[..., :, None] + second_norms[..., None, :] - 2.0 * inner_prod
    return jnp.exp(-rate_value * distance)


def local_tree(tree_points, tree_dir, skeleton, transfer, rate_value):
    leaves_here = tree_points.shape[0]
    leaf_kernel = kernel_block(skeleton[:leaves_here], tree_points, rate_value)
    upward_list = [jnp.einsum("lrp,lp->lr", leaf_kernel, tree_dir, precision=lax.Precision.HIGHEST)]
    coupled = []
    offset = 0
    width_now = leaves_here
    while width_now >= 2:
        node_skeleton = skeleton[offset:offset + width_now]
        flipped = jnp.flip(node_skeleton.reshape((width_now // 2, 2) + node_skeleton.shape[1:]), axis=1).reshape(node_skeleton.shape)
        values_flipped = jnp.flip(upward_list[-1].reshape(width_now // 2, 2, -1), axis=1).reshape(width_now, -1)
        couple_kernel = kernel_block(node_skeleton, flipped, rate_value)
        coupled.append(jnp.einsum("nrs,ns->nr", couple_kernel, values_flipped, precision=lax.Precision.HIGHEST))
        lifted = jnp.einsum("nrs,nr->ns", transfer[offset:offset + width_now].astype(jnp.float32), upward_list[-1], precision=lax.Precision.HIGHEST)
        upward_list.append((lifted[0::2] + lifted[1::2]) * half_root)
        offset = offset + width_now
        width_now = width_now // 2
    return leaf_kernel, upward_list[-1][0], coupled


def local_down(root_value, transfer, coupled):
    spans = []
    offset = 0
    for portion in coupled:
        spans.append((offset, portion.shape[0]))
        offset = offset + portion.shape[0]
    downward = root_value[None, :]
    for position in range(len(coupled) - 1, -1, -1):
        first_node, width_now = spans[position]
        parent = jnp.repeat(downward, 2, axis=0)
        downward = coupled[position] + jnp.einsum("nrs,ns->nr", transfer[first_node:first_node + width_now].astype(jnp.float32), parent, precision=lax.Precision.HIGHEST)
    return downward


def near_field(tree_points, extended, near_target, near_source, tile_total, first_leaf, own_first, rate_value):
    dims = tree_points.shape[1]
    leaves_here = tree_points.shape[0]

    def tile_block(block_id, running):
        slot_ids = block_id * 8 + jnp.arange(8, dtype=jnp.int32)
        target_rows = (lax.dynamic_slice_in_dim(near_target, block_id * 8, 8) - own_first).astype(jnp.int32)
        source_rows = (lax.dynamic_slice_in_dim(near_source, block_id * 8, 8) - first_leaf).astype(jnp.int32)
        alive_mask = (slot_ids < tile_total).astype(jnp.float32)
        target_pts = tree_points[target_rows]
        source_pack = extended[source_rows]
        block_kernel = kernel_block(target_pts, source_pack[:, :dims], rate_value)
        portion = jnp.einsum("bij,bj->bi", block_kernel, source_pack[:, dims], precision=lax.Precision.HIGHEST) * alive_mask[:, None]
        target_hot = (target_rows[:, None] == jnp.arange(leaves_here, dtype=jnp.int32)[None, :]).astype(jnp.float32)
        return running + jnp.einsum("bl,bi->li", target_hot, portion, precision=lax.Precision.HIGHEST)

    blocks = (tile_total + 7) // 8
    return lax.fori_loop(0, blocks, tile_block, jnp.zeros((leaves_here, tree_points.shape[2]), jnp.float32))


def reference(points, solution, residual, direction, ridge_weight, kernel_rate, tree_perm, local_skeleton, local_transfer, cross_skeleton, cross_transfer, near_target, near_source, tile_count):
    rate_value = kernel_rate[0]
    device_first = jnp.arange(N_LEAF, dtype=jnp.int32) * POINTS_DEV
    data_index = (tree_perm + device_first[:, None]).reshape(-1).astype(jnp.int32)
    tree_all = jnp.transpose(points[:, data_index].reshape(DIM, LEAVES, LEAF), (1, 0, 2))
    dir_all = direction[data_index].reshape(LEAVES, LEAF)
    packed_all = jnp.concatenate([tree_all, dir_all[:, None, :]], axis=1)
    tree_dev = tree_all.reshape(N_LEAF, LEAVES_DEV, DIM, LEAF)
    dir_dev = dir_all.reshape(N_LEAF, LEAVES_DEV, LEAF)
    skeleton_dev = local_skeleton.reshape(N_LEAF, LOCAL_NODES, DIM, RANK)
    transfer_dev = local_transfer.reshape(N_LEAF, LOCAL_NODES, RANK, RANK)

    def upward_root(inputs):
        return local_tree(inputs[0], inputs[1], inputs[2], inputs[3], rate_value)[1]

    node_values = lax.map(upward_root, (tree_dev, dir_dev, skeleton_dev, transfer_dev))
    skeleton_cross = cross_skeleton.reshape(N_LEAF, LEVELS_X, 2, DIM, RANK)
    transfer_cross = cross_transfer.reshape(N_LEAF, LEVELS_X - 1, 2, RANK, RANK)
    cross_values = []
    for level in range(LEVELS_X):
        stride = 2 ** level
        skeleton = skeleton_cross[::stride, level, 0]
        partner = jnp.arange(skeleton.shape[0], dtype=jnp.int32) ^ 1
        couple_kernel = kernel_block(skeleton, skeleton[partner], rate_value)
        cross_values.append(jnp.einsum("nrs,ns->nr", couple_kernel, node_values[partner], precision=lax.Precision.HIGHEST))
        if level < LEVELS_X - 1:
            transfer = transfer_cross[::stride, level, 0].astype(jnp.float32)
            lifted = jnp.einsum("nrs,nr->ns", transfer, node_values, precision=lax.Precision.HIGHEST)
            node_values = (lifted[0::2] + lifted[1::2]) * half_root
    current = cross_values[LEVELS_X - 1]
    for level in range(LEVELS_X - 2, -1, -1):
        transfer = transfer_cross[::2 ** level, level, 0].astype(jnp.float32)
        current = cross_values[level] + jnp.einsum("nrs,ns->nr", transfer, jnp.repeat(current, 2, axis=0), precision=lax.Precision.HIGHEST)
    targets_dev = near_target.reshape(N_LEAF, TILE_CAP)
    sources_dev = near_source.reshape(N_LEAF, TILE_CAP)
    device_ids = jnp.arange(N_LEAF, dtype=jnp.int32)

    def device_image(inputs):
        tree_points, tree_dir, skeleton, transfer, root_down, targets, sources, tile_total, device_id = inputs
        leaf_kernel, root_value, coupled = local_tree(tree_points, tree_dir, skeleton, transfer, rate_value)
        downward = local_down(root_down, transfer, coupled)
        far = jnp.einsum("lrp,lr->lp", leaf_kernel, downward, precision=lax.Precision.HIGHEST)
        near = near_field(tree_points, packed_all, targets, sources, tile_total, 0, device_id * LEAVES_DEV, rate_value)
        return ridge_weight[0] * tree_dir + near + far

    image_tree = lax.map(device_image, (tree_dev, dir_dev, skeleton_dev, transfer_dev, current, targets_dev, sources_dev, tile_count, device_ids))
    image = jnp.zeros((POINTS,), jnp.float32).at[data_index].set(image_tree.reshape(-1))
    norm_old = jnp.sum(residual * residual)
    curvature = jnp.sum(direction * image)
    step_size = norm_old / curvature
    new_solution = solution + step_size * direction
    new_residual = residual - step_size * image
    norm_new = jnp.sum(new_residual * new_residual)
    new_direction = new_residual + (norm_new / (norm_old + epsilon)) * direction
    return new_solution, new_residual, new_direction
```

```python
import functools
import math

import jax
import jax.numpy as jnp
from jax import lax
from jax.experimental import pallas as pl
from jax.experimental.pallas import tpu as pltpu
from jax.sharding import PartitionSpec as P

LEAF = 256
LEAVES_DEV = 32
REACH = 16
DIM = 32
NODES = 62
WAYS = 4

epsilon = 1e-06
half_root = 0.5**0.5
LOG2E = math.log2(math.e)
F32 = jnp.float32
BF16 = jnp.bfloat16
VMEM = pl.BlockSpec(memory_space=pltpu.VMEM)
SMEM = pl.BlockSpec(memory_space=pltpu.SMEM)


def split(value, count):
    parts = []
    for _ in range(count):
        part = value.astype(BF16).astype(F32)
        parts.append(part)
        value = value - part
    return parts


def norm_row(pts, rate):
    return jnp.sum(pts * pts, axis=0, keepdims=True) * (-rate * LOG2E)


def row_stack(pts, norm):
    high, low = split(pts, 2)
    one = jnp.ones_like(norm)
    width = pts.shape[1]
    tail = jnp.concatenate(split(norm, 3) + [one] * 3 + [jnp.zeros((26, width), F32)], axis=0)
    return jnp.concatenate([high, high, low, tail], axis=0)


def col_stack(pts, norm, rate):
    high, low = split(pts * (2.0 * LOG2E * rate), 2)
    one = jnp.ones_like(norm)
    width = pts.shape[1]
    tail = jnp.concatenate([one] * 3 + split(norm, 3) + [jnp.zeros((26, width), F32)], axis=0)
    return jnp.concatenate([high, low, high, tail], axis=0).astype(BF16)


def tile(rows, cols):
    return jnp.exp2(jnp.dot(rows, cols, preferred_element_type=F32))


def split_rows(row):
    return jnp.concatenate(
        split(row, 3) + [jnp.zeros((13, row.shape[1]), F32)], axis=0
    ).astype(BF16)


LEVELS = []
_first, _width = 0, LEAVES_DEV
while _width >= 2:
    LEVELS.append((_first, _width))
    _first, _width = _first + _width, _width // 2


def up_kernel(perm, rate_ref, pts, dirs, skel, trans, gt, rows_out, ups, raw, held):
    rate = rate_ref[0]
    blocks = pts.shape[1] // 128

    def place(block, _):
        at = pl.multiple_of(block * 128, 128)
        part = pts[:, pl.ds(at, 128)]
        stacked = jnp.concatenate(
            [part, dirs[pl.ds(block, 1), :], norm_row(part, rate), jnp.zeros((94, 128), F32)],
            axis=0,
        )
        raw[pl.ds(at, 128), :] = stacked.T
        return 0

    lax.fori_loop(0, blocks, place, 0, unroll=2)

    def gather(group, _):
        base = pl.multiple_of(group * 32, 32)
        for i in range(32):
            held[pl.ds(base + i, 1), :] = raw[pl.ds(perm[base + i], 1), :]
        return 0

    lax.fori_loop(0, pts.shape[1] // 32, gather, 0)

    def leaf(j, _):
        at = pl.multiple_of(j * LEAF, LEAF)
        mine = held[pl.ds(at, LEAF), :]
        turned = mine.T
        gt[:, pl.ds(at, LEAF)] = turned[:40]
        rows = row_stack(turned[:32], turned[33:34]).T.astype(BF16)
        rows_out[j] = rows
        node = skel[j]
        kern = tile(rows, col_stack(node, norm_row(node, rate), rate))
        ups[pl.ds(j, 1), :] = jnp.sum(kern * mine[:, 32:33], axis=0, keepdims=True)
        return 0

    lax.fori_loop(0, LEAVES_DEV, leaf, 0, unroll=2)

    for first, width in LEVELS:
        for i in range(width // 2):
            total = jnp.zeros((16, LEAF), F32)
            for node in (first + 2 * i, first + 2 * i + 1):
                total = total + jnp.dot(
                    split_rows(ups[node : node + 1, :]), trans[node], preferred_element_type=F32
                )
            ups[first + width + i : first + width + i + 1, :] = (
                jnp.sum(total, axis=0, keepdims=True) * half_root
            )
    ups[63:64, :] = jnp.zeros((1, LEAF), F32)


def down_kernel(
    tgt, src, cnt, first_ref, rate_ref, ridge_ref, perm, gt, left, right, rows, ups, root,
    skel, trans, image, cols, dirs, acc, couple, turned_img,
):
    rate = rate_ref[0]
    first = first_ref[0]

    def load_cols(ref, base):
        def body(i, _):
            at = pl.multiple_of(i * LEAF, LEAF)
            cols[base + i] = col_stack(ref[0:32, pl.ds(at, LEAF)], ref[33:34, pl.ds(at, LEAF)], rate)
            dirs[base + i] = jnp.broadcast_to(ref[32:33, pl.ds(at, LEAF)], (8, LEAF))
            return 0

        lax.fori_loop(0, ref.shape[1] // LEAF, body, 0, unroll=2)

    load_cols(left, 0)
    load_cols(gt, REACH)
    load_cols(right, REACH + LEAVES_DEV)

    lane = lax.broadcasted_iota(jnp.int32, (LEAF, 128), 1)
    couple[...] = jnp.zeros_like(couple)

    def pair(i, _):
        for a, b in ((2 * i, 2 * i + 1), (2 * i + 1, 2 * i)):
            mine, other = skel[a], skel[b]
            kern = tile(
                row_stack(mine, norm_row(mine, rate)).T.astype(BF16),
                col_stack(other, norm_row(other, rate), rate),
            )
            value = jnp.sum(kern * ups[pl.ds(b, 1), :], axis=1, keepdims=True)
            couple[...] = jnp.where(lane == a, value, couple[...])
        return 0

    lax.fori_loop(0, NODES // 2, pair, 0)
    coupled = couple[...].T

    down = {NODES: root[...]}
    for level in range(len(LEVELS) - 1, -1, -1):
        start, width = LEVELS[level]
        for i in range(width // 2):
            parts = split_rows(down[start + width + i])
            for node in (start + 2 * i, start + 2 * i + 1):
                moved = lax.dot_general(
                    parts, trans[node], (((1,), (1,)), ((), ())), preferred_element_type=F32
                )
                down[node] = coupled[node : node + 1] + jnp.sum(moved, axis=0, keepdims=True)
    couple[0:LEAVES_DEV, :] = jnp.concatenate(
        [down[j][:, 0:128] for j in range(LEAVES_DEV)], axis=0
    )
    couple[LEAVES_DEV : 2 * LEAVES_DEV, :] = jnp.concatenate(
        [down[j][:, 128:256] for j in range(LEAVES_DEV)], axis=0
    )

    def far(j, _):
        node = skel[j]
        kern = tile(rows[j], col_stack(node, norm_row(node, rate), rate))
        acc[0, j] = (
            kern[:, 0:128] * couple[pl.ds(j, 1), :]
            + kern[:, 128:256] * couple[pl.ds(j + LEAVES_DEV, 1), :]
        )
        for way in range(1, WAYS):
            acc[way, j] = jnp.zeros((LEAF, 128), F32)
        return 0

    lax.fori_loop(0, LEAVES_DEV, far, 0, unroll=2)

    total = cnt[0]

    def near(step, _):
        for way in range(WAYS):
            slot = step * WAYS + way
            target = jnp.clip(tgt[slot] - first, 0, LEAVES_DEV - 1)
            source = jnp.clip(src[slot] - first + REACH, 0, LEAVES_DEV + 2 * REACH - 1)
            weight = jnp.where(slot < total, dirs[source][0:1, :], 0.0)
            kern = tile(rows[target], cols[source]) * weight
            acc[way, target] += kern[:, 0:128] + kern[:, 128:256]
        return 0

    lax.fori_loop(0, (total + WAYS - 1) // WAYS, near, 0)

    turned_img[...] = jnp.zeros_like(turned_img)

    def gather_image(j, _):
        value = acc[0, j]
        for way in range(1, WAYS):
            value = value + acc[way, j]
        turned_img[...] = jnp.where(
            lane == j, jnp.sum(value, axis=1, keepdims=True), turned_img[...]
        )
        return 0

    lax.fori_loop(0, LEAVES_DEV, gather_image, 0)
    tree_image = turned_img[...].T

    grand = jnp.zeros((192, 128), F32)
    high_id = lax.broadcasted_iota(jnp.int32, (64, LEAF), 0)
    low_id = lax.broadcasted_iota(jnp.int32, (128, LEAF), 0)
    for j in range(LEAVES_DEV):
        at = perm[j : j + 1, :]
        value = tree_image[j : j + 1, :] + ridge_ref[0] * dirs[REACH + j][0:1, :]
        hot = high_id == (at >> 7)
        picked = jnp.concatenate(
            [jnp.where(hot, part, 0.0) for part in split(value, 3)], axis=0
        ).astype(BF16)
        low = jnp.where(low_id == (at & 127), 1.0, 0.0).astype(BF16)
        grand = grand + lax.dot_general(
            picked, low, (((1,), (1,)), ((), ())), preferred_element_type=F32
        )
    image[...] = grand[0:64] + grand[64:128] + grand[128:192]


PARAMS = pltpu.CompilerParams(vmem_limit_bytes=60 * 1024 * 1024)


def call_up(perm, rate, points, direction, skeleton, transfer):
    count = points.shape[1]
    return pl.pallas_call(
        up_kernel,
        out_shape=(
            jax.ShapeDtypeStruct((40, count), F32),
            jax.ShapeDtypeStruct((LEAVES_DEV, LEAF, 128), BF16),
            jax.ShapeDtypeStruct((64, LEAF), F32),
        ),
        in_specs=[SMEM, SMEM, VMEM, VMEM, VMEM, VMEM],
        out_specs=(VMEM, VMEM, VMEM),
        scratch_shapes=[pltpu.VMEM((count, 128), F32), pltpu.VMEM((count, 128), F32)],
        compiler_params=PARAMS,
        name="up_tree",
    )(perm, rate, points, direction, skeleton, transfer)


def call_down(tgt, src, cnt, first, rate, ridge, perm, gt, left, right, rows, ups, root, skel, trans):
    return pl.pallas_call(
        down_kernel,
        out_shape=jax.ShapeDtypeStruct((64, 128), F32),
        in_specs=[SMEM] * 6 + [VMEM] * 9,
        out_specs=VMEM,
        scratch_shapes=[
            pltpu.VMEM((LEAVES_DEV + 2 * REACH, 128, LEAF), BF16),
            pltpu.VMEM((LEAVES_DEV + 2 * REACH, 8, LEAF), F32),
            pltpu.VMEM((WAYS, LEAVES_DEV, LEAF, 128), F32),
            pltpu.VMEM((LEAF, 128), F32),
            pltpu.VMEM((LEAF, 128), F32),
        ],
        compiler_params=PARAMS,
        name="down_near",
    )(tgt, src, cnt, first, rate, ridge, perm, gt, left, right, rows, ups, root, skel, trans)


def partner(value, axis, distance):
    mask = 2**distance
    pairs = [(source, source ^ mask) for source in range(lax.axis_size(axis))]
    return lax.ppermute(value, axis, pairs)


def kernel_block(first_set, second_set, rate_value):
    first_norms = jnp.sum(first_set * first_set, axis=-2)
    second_norms = jnp.sum(second_set * second_set, axis=-2)
    inner_prod = jnp.einsum(
        "...dm,...dn->...mn", first_set, second_set, precision=lax.Precision.HIGHEST
    )
    distance = first_norms[..., :, None] + second_norms[..., None, :] - 2.0 * inner_prod
    return jnp.exp(-rate_value * distance)


def shards(
    points,
    solution,
    residual,
    direction,
    ridge_weight,
    kernel_rate,
    tree_perm,
    local_skeleton,
    local_transfer,
    cross_skeleton,
    cross_transfer,
    near_target,
    near_source,
    tile_count,
):
    rate_value = kernel_rate[0]
    devices = lax.axis_size("leaf")
    device_index = lax.axis_index("leaf")
    gt, rows, ups = call_up(
        tree_perm[0], kernel_rate, points, direction.reshape(64, 128), local_skeleton, local_transfer
    )
    edge = REACH * LEAF
    onward = [(i, (i + 1) % devices) for i in range(devices - 1)]
    back = [(j, i) for i, j in onward]
    left = lax.ppermute(gt[:, gt.shape[1] - edge :], "leaf", onward)
    right = lax.ppermute(gt[:, :edge], "leaf", back)
    levels = devices.bit_length() - 1
    couple_kernel = kernel_block(cross_skeleton[:, 0], cross_skeleton[:, 1], rate_value)
    own_transfer = cross_transfer[:, 0].astype(jnp.float32)
    current = ups[NODES]
    sibling_list = []
    for level in range(levels):
        sibling_value = partner(current, "leaf", level)
        sibling_list.append(sibling_value)
        if level < levels - 1:
            mine_lift = jnp.dot(current, own_transfer[level], precision=lax.Precision.HIGHEST)
            other_lift = jnp.dot(
                sibling_value,
                cross_transfer[level, 1].astype(jnp.float32),
                precision=lax.Precision.HIGHEST,
            )
            current = (mine_lift + other_lift) * half_root
    sibling_values = jnp.stack(sibling_list)
    cross_values = jnp.einsum(
        "lrs,ls->lr", couple_kernel, sibling_values, precision=lax.Precision.HIGHEST
    )
    current = cross_values[levels - 1]
    for level in range(levels - 2, -1, -1):
        current = cross_values[level] + jnp.dot(
            own_transfer[level], current, precision=lax.Precision.HIGHEST
        )
    own_first = (device_index * LEAVES_DEV).astype(jnp.int32).reshape(1)
    image = call_down(
        near_target, near_source, tile_count, own_first, kernel_rate, ridge_weight,
        tree_perm.reshape(LEAVES_DEV, LEAF), gt, left, right, rows, ups, current.reshape(1, LEAF),
        local_skeleton, local_transfer,
    ).reshape(-1)
    norm_old, curvature = lax.psum(
        (jnp.sum(residual * residual), jnp.sum(direction * image)), "leaf"
    )
    step_size = norm_old / curvature
    new_residual = residual - step_size * image
    norm_new = lax.psum(jnp.sum(new_residual * new_residual), "leaf")
    new_solution = solution + step_size * direction
    new_direction = new_residual + norm_new / (norm_old + epsilon) * direction
    return (new_solution, new_residual, new_direction)


def solution(mesh):
    return jax.shard_map(
        shards,
        mesh=mesh,
        in_specs=(
            P(None, ("groups", "leaf")),
            P(("groups", "leaf")),
            P(("groups", "leaf")),
            P(("groups", "leaf")),
            P("groups"),
            P("groups"),
            P(("groups", "leaf"), None),
            P(("groups", "leaf"), None, None),
            P(("groups", "leaf"), None, None),
            P(("groups", "leaf"), None, None, None),
            P(("groups", "leaf"), None, None, None),
            P(("groups", "leaf")),
            P(("groups", "leaf")),
            P(("groups", "leaf")),
        ),
        out_specs=(P(("groups", "leaf")), P(("groups", "leaf")), P(("groups", "leaf"))),
        check_vma=False,
    )
```

```python
import functools
import math

import jax
import jax.numpy as jnp
from jax import lax
from jax.experimental import pallas as pl
from jax.experimental.pallas import tpu as pltpu
from jax.sharding import PartitionSpec as P

LEAF = 256
LEAVES_DEV = 32
REACH = 16
DIM = 32
NODES = 62
WAYS = 4

epsilon = 1e-06
half_root = 0.5**0.5
LOG2E = math.log2(math.e)
F32 = jnp.float32
BF16 = jnp.bfloat16
VMEM = pl.BlockSpec(memory_space=pltpu.VMEM)
SMEM = pl.BlockSpec(memory_space=pltpu.SMEM)


def split(value, count):
    parts = []
    for _ in range(count):
        part = value.astype(BF16).astype(F32)
        parts.append(part)
        value = value - part
    return parts


def norm_row(pts, rate):
    return jnp.sum(pts * pts, axis=0, keepdims=True) * (-rate * LOG2E)


def row_stack(pts, norm):
    high, low = split(pts, 2)
    one = jnp.ones_like(norm)
    width = pts.shape[1]
    tail = jnp.concatenate(split(norm, 3) + [one] * 3 + [jnp.zeros((26, width), F32)], axis=0)
    return jnp.concatenate([high, high, low, tail], axis=0)


def col_stack(pts, norm, rate):
    high, low = split(pts * (2.0 * LOG2E * rate), 2)
    one = jnp.ones_like(norm)
    width = pts.shape[1]
    tail = jnp.concatenate([one] * 3 + split(norm, 3) + [jnp.zeros((26, width), F32)], axis=0)
    return jnp.concatenate([high, low, high, tail], axis=0).astype(BF16)


def tile(rows, cols):
    return jnp.exp2(jnp.dot(rows, cols, preferred_element_type=F32))


def split_rows(row):
    return jnp.concatenate(
        split(row, 3) + [jnp.zeros((13, row.shape[1]), F32)], axis=0
    ).astype(BF16)


LEVELS = []
_first, _width = 0, LEAVES_DEV
while _width >= 2:
    LEVELS.append((_first, _width))
    _first, _width = _first + _width, _width // 2


def up_kernel(perm, rate_ref, pts, dirs, skel, trans, gt, rows_out, ups, raw, held):
    rate = rate_ref[0]
    blocks = pts.shape[1] // 128

    def place(block, _):
        at = pl.multiple_of(block * 128, 128)
        part = pts[:, pl.ds(at, 128)]
        stacked = jnp.concatenate(
            [part, dirs[pl.ds(block, 1), :], norm_row(part, rate), jnp.zeros((94, 128), F32)],
            axis=0,
        )
        raw[pl.ds(at, 128), :] = stacked.T
        return 0

    lax.fori_loop(0, blocks, place, 0, unroll=2)

    def gather(group, _):
        base = pl.multiple_of(group * 32, 32)
        for i in range(32):
            held[pl.ds(base + i, 1), :] = raw[pl.ds(perm[base + i], 1), :]
        return 0

    lax.fori_loop(0, pts.shape[1] // 32, gather, 0)

    def leaf(j, _):
        at = pl.multiple_of(j * LEAF, LEAF)
        mine = held[pl.ds(at, LEAF), :]
        turned = mine.T
        gt[:, pl.ds(at, LEAF)] = turned[:40]
        rows = row_stack(turned[:32], turned[33:34]).T.astype(BF16)
        rows_out[j] = rows
        node = skel[j]
        kern = tile(rows, col_stack(node, norm_row(node, rate), rate))
        ups[pl.ds(j, 1), :] = jnp.sum(kern * mine[:, 32:33], axis=0, keepdims=True)
        return 0

    lax.fori_loop(0, LEAVES_DEV, leaf, 0, unroll=2)

    for first, width in LEVELS:
        for i in range(width // 2):
            total = jnp.zeros((16, LEAF), F32)
            for node in (first + 2 * i, first + 2 * i + 1):
                total = total + jnp.dot(
                    split_rows(ups[node : node + 1, :]), trans[node], preferred_element_type=F32
                )
            ups[first + width + i : first + width + i + 1, :] = (
                jnp.sum(total, axis=0, keepdims=True) * half_root
            )
    ups[63:64, :] = jnp.zeros((1, LEAF), F32)


def down_kernel(
    tgt, src, cnt, first_ref, rate_ref, ridge_ref, perm, gt, left, right, rows, ups, root,
    skel, trans, image, cols, dirs, acc, couple, turned_img,
):
    rate = rate_ref[0]
    first = first_ref[0]

    def load_cols(ref, base):
        def body(i, _):
            at = pl.multiple_of(i * LEAF, LEAF)
            cols[base + i] = col_stack(ref[0:32, pl.ds(at, LEAF)], ref[33:34, pl.ds(at, LEAF)], rate)
            dirs[base + i] = jnp.broadcast_to(ref[32:33, pl.ds(at, LEAF)], (8, LEAF))
            return 0

        lax.fori_loop(0, ref.shape[1] // LEAF, body, 0, unroll=2)

    load_cols(left, 0)
    load_cols(gt, REACH)
    load_cols(right, REACH + LEAVES_DEV)

    lane = lax.broadcasted_iota(jnp.int32, (LEAF, 128), 1)
    couple[...] = jnp.zeros_like(couple)

    def pair(i, _):
        for a, b in ((2 * i, 2 * i + 1), (2 * i + 1, 2 * i)):
            mine, other = skel[a], skel[b]
            kern = tile(
                row_stack(mine, norm_row(mine, rate)).T.astype(BF16),
                col_stack(other, norm_row(other, rate), rate),
            )
            value = jnp.sum(kern * ups[pl.ds(b, 1), :], axis=1, keepdims=True)
            couple[...] = jnp.where(lane == a, value, couple[...])
        return 0

    lax.fori_loop(0, NODES // 2, pair, 0)
    coupled = couple[...].T

    down = {NODES: root[...]}
    for level in range(len(LEVELS) - 1, -1, -1):
        start, width = LEVELS[level]
        for i in range(width // 2):
            parts = split_rows(down[start + width + i])
            for node in (start + 2 * i, start + 2 * i + 1):
                moved = lax.dot_general(
                    parts, trans[node], (((1,), (1,)), ((), ())), preferred_element_type=F32
                )
                down[node] = coupled[node : node + 1] + jnp.sum(moved, axis=0, keepdims=True)
    couple[0:LEAVES_DEV, :] = jnp.concatenate(
        [down[j][:, 0:128] for j in range(LEAVES_DEV)], axis=0
    )
    couple[LEAVES_DEV : 2 * LEAVES_DEV, :] = jnp.concatenate(
        [down[j][:, 128:256] for j in range(LEAVES_DEV)], axis=0
    )

    def far(j, _):
        node = skel[j]
        kern = tile(rows[j], col_stack(node, norm_row(node, rate), rate))
        acc[0, j] = (
            kern[:, 0:128] * couple[pl.ds(j, 1), :]
            + kern[:, 128:256] * couple[pl.ds(j + LEAVES_DEV, 1), :]
        )
        for way in range(1, WAYS):
            acc[way, j] = jnp.zeros((LEAF, 128), F32)
        return 0

    lax.fori_loop(0, LEAVES_DEV, far, 0, unroll=2)

    total = cnt[0]

    def near(step, _):
        for way in range(WAYS):
            slot = step * WAYS + way
            target = jnp.clip(tgt[slot] - first, 0, LEAVES_DEV - 1)
            source = jnp.clip(src[slot] - first + REACH, 0, LEAVES_DEV + 2 * REACH - 1)
            source = jnp.where(slot < total, source, target + REACH)
            weight = jnp.where(slot < total, dirs[source][0:1, :], 0.0)
            kern = tile(rows[target], cols[source]) * weight
            acc[way, target] += kern[:, 0:128] + kern[:, 128:256]
        return 0

    lax.fori_loop(0, (total + WAYS - 1) // WAYS, near, 0)

    turned_img[...] = jnp.zeros_like(turned_img)

    def gather_image(j, _):
        value = acc[0, j]
        for way in range(1, WAYS):
            value = value + acc[way, j]
        turned_img[...] = jnp.where(
            lane == j, jnp.sum(value, axis=1, keepdims=True), turned_img[...]
        )
        return 0

    lax.fori_loop(0, LEAVES_DEV, gather_image, 0)
    tree_image = turned_img[...].T

    grand = jnp.zeros((192, 128), F32)
    high_id = lax.broadcasted_iota(jnp.int32, (64, LEAF), 0)
    low_id = lax.broadcasted_iota(jnp.int32, (128, LEAF), 0)
    for j in range(LEAVES_DEV):
        at = perm[j : j + 1, :]
        value = tree_image[j : j + 1, :] + ridge_ref[0] * dirs[REACH + j][0:1, :]
        hot = high_id == (at >> 7)
        picked = jnp.concatenate(
            [jnp.where(hot, part, 0.0) for part in split(value, 3)], axis=0
        ).astype(BF16)
        low = jnp.where(low_id == (at & 127), 1.0, 0.0).astype(BF16)
        grand = grand + lax.dot_general(
            picked, low, (((1,), (1,)), ((), ())), preferred_element_type=F32
        )
    image[...] = grand[0:64] + grand[64:128] + grand[128:192]


PARAMS = pltpu.CompilerParams(vmem_limit_bytes=60 * 1024 * 1024)


def call_up(perm, rate, points, direction, skeleton, transfer):
    count = points.shape[1]
    return pl.pallas_call(
        up_kernel,
        out_shape=(
            jax.ShapeDtypeStruct((40, count), F32),
            jax.ShapeDtypeStruct((LEAVES_DEV, LEAF, 128), BF16),
            jax.ShapeDtypeStruct((64, LEAF), F32),
        ),
        in_specs=[SMEM, SMEM, VMEM, VMEM, VMEM, VMEM],
        out_specs=(VMEM, VMEM, VMEM),
        scratch_shapes=[pltpu.VMEM((count, 128), F32), pltpu.VMEM((count, 128), F32)],
        compiler_params=PARAMS,
        name="up_tree",
    )(perm, rate, points, direction, skeleton, transfer)


def call_down(tgt, src, cnt, first, rate, ridge, perm, gt, left, right, rows, ups, root, skel, trans):
    return pl.pallas_call(
        down_kernel,
        out_shape=jax.ShapeDtypeStruct((64, 128), F32),
        in_specs=[SMEM] * 6 + [VMEM] * 9,
        out_specs=VMEM,
        scratch_shapes=[
            pltpu.VMEM((LEAVES_DEV + 2 * REACH, 128, LEAF), BF16),
            pltpu.VMEM((LEAVES_DEV + 2 * REACH, 8, LEAF), F32),
            pltpu.VMEM((WAYS, LEAVES_DEV, LEAF, 128), F32),
            pltpu.VMEM((LEAF, 128), F32),
            pltpu.VMEM((LEAF, 128), F32),
        ],
        compiler_params=PARAMS,
        name="down_near",
    )(tgt, src, cnt, first, rate, ridge, perm, gt, left, right, rows, ups, root, skel, trans)


def remote_params(collective_id):
    return pltpu.CompilerParams(
        vmem_limit_bytes=60 * 1024 * 1024, collective_id=collective_id, has_side_effects=True
    )


def signal(barrier, device):
    pl.semaphore_signal(
        barrier, inc=1, device_id={"leaf": device}, device_id_type=pl.DeviceIdType.MESH
    )


def remote(src, dst, send_sem, recv_sem, device):
    return pltpu.make_async_remote_copy(
        src_ref=src,
        dst_ref=dst,
        send_sem=send_sem,
        recv_sem=recv_sem,
        device_id={"leaf": device},
        device_id_type=pl.DeviceIdType.MESH,
    )


def cross_kernel(
    devices, rate_ref, ups, skel, trans, gt, down, left, right,
    sent, slots, kerns, couple, halo_send, halo_recv, hop_send, hop_recv,
):
    rate = rate_ref[0]
    me = lax.axis_index("leaf")
    levels = skel.shape[0]
    edge = left.shape[1]
    peers = []
    for level in range(levels):
        mask = 2**level
        peers.append(me + mask * (1 - 2 * ((me // mask) % 2)))
    has_left, has_right = me > 0, me < devices - 1

    barrier = pltpu.get_barrier_semaphore()
    for peer in peers:
        signal(barrier, peer)
    for present, peer in ((has_left, me - 1), (has_right, me + 1)):

        @pl.when(present)
        def _():
            signal(barrier, peer)

    pl.semaphore_wait(
        barrier, levels + has_left.astype(jnp.int32) + has_right.astype(jnp.int32)
    )

    def hop(level):
        return remote(
            sent.at[level], slots.at[level], hop_send.at[level], hop_recv.at[level], peers[level]
        )

    to_left = remote(
        gt.at[:, pl.ds(0, edge)], right, halo_send.at[0], halo_recv.at[0], me - 1
    )
    to_right = remote(
        gt.at[:, pl.ds(gt.shape[1] - edge, edge)], left, halo_send.at[1], halo_recv.at[1], me + 1
    )

    current = ups[NODES : NODES + 1, :]
    sent[0] = jnp.broadcast_to(current, (8, LEAF))
    hop(0).start()
    pl.when(has_left)(to_left.start)
    pl.when(has_right)(to_right.start)

    def couplings(level, _):
        mine, other = skel[level, 0], skel[level, 1]
        kerns[level] = tile(
            row_stack(mine, norm_row(mine, rate)).T.astype(BF16),
            col_stack(other, norm_row(other, rate), rate),
        )
        return 0

    lax.fori_loop(0, levels, couplings, 0)
    for level in range(levels):
        hop(level).wait()
        if level < levels - 1:
            total = jnp.dot(
                split_rows(current), trans[level, 0], preferred_element_type=F32
            ) + jnp.dot(
                split_rows(slots[level][0:1]), trans[level, 1], preferred_element_type=F32
            )
            current = jnp.sum(total, axis=0, keepdims=True) * half_root
            sent[level + 1] = jnp.broadcast_to(current, (8, LEAF))
            hop(level + 1).start()
    lane = lax.broadcasted_iota(jnp.int32, (LEAF, 128), 1)
    picked = jnp.zeros((LEAF, 128), F32)
    for level in range(levels):
        value = jnp.sum(kerns[level] * slots[level][0:1], axis=1, keepdims=True)
        picked = jnp.where(lane == level, value, picked)
    couple[...] = picked.T
    current = couple[levels - 1 : levels, :]
    for level in range(levels - 2, -1, -1):
        moved = lax.dot_general(
            split_rows(current), trans[level, 0], (((1,), (1,)), ((), ())),
            preferred_element_type=F32,
        )
        current = couple[level : level + 1, :] + jnp.sum(moved, axis=0, keepdims=True)
    down[...] = current

    @pl.when(has_left)
    def _():
        to_left.wait_send()
        to_right.wait_recv()

    @pl.when(has_right)
    def _():
        to_right.wait_send()
        to_left.wait_recv()


def call_cross(devices, rate, ups, skel, trans, gt):
    levels = skel.shape[0]
    edge = REACH * LEAF
    return pl.pallas_call(
        functools.partial(cross_kernel, devices),
        out_shape=(
            jax.ShapeDtypeStruct((1, LEAF), F32),
            jax.ShapeDtypeStruct((40, edge), F32),
            jax.ShapeDtypeStruct((40, edge), F32),
        ),
        in_specs=[SMEM, VMEM, VMEM, VMEM, pl.BlockSpec(memory_space=pl.ANY)],
        out_specs=(
            VMEM, pl.BlockSpec(memory_space=pl.ANY), pl.BlockSpec(memory_space=pl.ANY),
        ),
        scratch_shapes=[
            pltpu.VMEM((levels, 8, LEAF), F32),
            pltpu.VMEM((levels, 8, LEAF), F32),
            pltpu.VMEM((levels, LEAF, LEAF), F32),
            pltpu.VMEM((128, LEAF), F32),
            pltpu.SemaphoreType.DMA((2,)),
            pltpu.SemaphoreType.DMA((2,)),
            pltpu.SemaphoreType.DMA((levels,)),
            pltpu.SemaphoreType.DMA((levels,)),
        ],
        compiler_params=remote_params(0),
        name="cross_levels",
    )(rate, ups, skel, trans, gt)


def step_kernel(
    devices, image, solution, residual, direction, new_solution, new_residual, new_direction,
    sent, slots, send_sem, recv_sem,
):
    me = lax.axis_index("leaf")
    barrier = pltpu.get_barrier_semaphore()

    def greet(offset, _):
        signal(barrier, (me + offset) % devices)
        return 0

    lax.fori_loop(1, devices, greet, 0)
    res, dire, img = residual[...], direction[...], image[...]
    sent[0] = jnp.concatenate(
        [
            jnp.sum(res * res, axis=0, keepdims=True),
            jnp.sum(dire * img, axis=0, keepdims=True),
            jnp.zeros((6, 128), F32),
        ],
        axis=0,
    )
    pl.semaphore_wait(barrier, devices - 1)

    def total(phase):
        def copy(offset):
            return remote(
                sent.at[phase],
                slots.at[phase, offset],
                send_sem.at[phase, offset],
                recv_sem.at[phase, offset],
                (me + offset) % devices,
            )

        def start(offset, _):
            copy(offset).start()
            return 0

        def finish(offset, running):
            copy(offset).wait()
            return running + slots[phase, offset]

        lax.fori_loop(1, devices, start, 0)
        lanes = lax.fori_loop(1, devices, finish, sent[phase])
        return jnp.sum(lanes, axis=1, keepdims=True)

    sums = total(0)
    norm_old = sums[0:1]
    step_size = norm_old / sums[1:2]
    new_res = res - step_size * img
    new_residual[...] = new_res
    sent[1] = jnp.concatenate(
        [jnp.sum(new_res * new_res, axis=0, keepdims=True), jnp.zeros((7, 128), F32)], axis=0
    )
    norm_new = total(1)[0:1]
    new_solution[...] = solution[...] + step_size * dire
    new_direction[...] = new_res + norm_new / (norm_old + epsilon) * dire


def call_step(devices, image, solution, residual, direction):
    flat = jax.ShapeDtypeStruct((64, 128), F32)
    return pl.pallas_call(
        functools.partial(step_kernel, devices),
        out_shape=(flat, flat, flat),
        in_specs=[VMEM] * 4,
        out_specs=(VMEM,) * 3,
        scratch_shapes=[
            pltpu.VMEM((2, 8, 128), F32),
            pltpu.VMEM((2, devices, 8, 128), F32),
            pltpu.SemaphoreType.DMA((2, devices)),
            pltpu.SemaphoreType.DMA((2, devices)),
        ],
        compiler_params=remote_params(1),
        name="step",
    )(image, solution, residual, direction)


def shards(
    points,
    solution,
    residual,
    direction,
    ridge_weight,
    kernel_rate,
    tree_perm,
    local_skeleton,
    local_transfer,
    cross_skeleton,
    cross_transfer,
    near_target,
    near_source,
    tile_count,
):
    devices = lax.axis_size("leaf")
    folded = tuple(array.reshape(64, 128) for array in (solution, residual, direction))
    gt, rows, ups = call_up(
        tree_perm[0], kernel_rate, points, folded[2], local_skeleton, local_transfer
    )
    root, left, right = call_cross(
        devices, kernel_rate, ups, cross_skeleton, cross_transfer, gt
    )
    own_first = (lax.axis_index("leaf") * LEAVES_DEV).astype(jnp.int32).reshape(1)
    image = call_down(
        near_target, near_source, tile_count, own_first, kernel_rate, ridge_weight,
        tree_perm.reshape(LEAVES_DEV, LEAF), gt, left, right, rows, ups, root,
        local_skeleton, local_transfer,
    )
    return tuple(array.reshape(-1) for array in call_step(devices, image, *folded))


def solution(mesh):
    return jax.shard_map(
        shards,
        mesh=mesh,
        in_specs=(
            P(None, ("groups", "leaf")),
            P(("groups", "leaf")),
            P(("groups", "leaf")),
            P(("groups", "leaf")),
            P("groups"),
            P("groups"),
            P(("groups", "leaf"), None),
            P(("groups", "leaf"), None, None),
            P(("groups", "leaf"), None, None),
            P(("groups", "leaf"), None, None, None),
            P(("groups", "leaf"), None, None, None),
            P(("groups", "leaf")),
            P(("groups", "leaf")),
            P(("groups", "leaf")),
        ),
        out_specs=(P(("groups", "leaf")), P(("groups", "leaf")), P(("groups", "leaf"))),
        check_vma=False,
    )
```

```python
import functools
import math

import jax
import jax.numpy as jnp
from jax import lax
from jax.experimental import pallas as pl
from jax.experimental.pallas import tpu as pltpu
from jax.sharding import PartitionSpec as P

LEAF = 256
LEAVES_DEV = 32
REACH = 16
DIM = 32
NODES = 62
WAYS = 4

epsilon = 1e-06
half_root = 0.5**0.5
LOG2E = math.log2(math.e)
F32 = jnp.float32
BF16 = jnp.bfloat16
VMEM = pl.BlockSpec(memory_space=pltpu.VMEM)
SMEM = pl.BlockSpec(memory_space=pltpu.SMEM)


def split(value, count):
    parts = []
    for _ in range(count):
        part = value.astype(BF16).astype(F32)
        parts.append(part)
        value = value - part
    return parts


def norm_row(pts, rate):
    return jnp.sum(pts * pts, axis=0, keepdims=True) * (-rate * LOG2E)


def row_stack(pts, norm, value):
    high, low = split(pts, 2)
    one = jnp.ones_like(norm)
    width = pts.shape[1]
    tail = jnp.concatenate(
        split(norm, 3)
        + [one] * 3
        + [jnp.zeros((10, width), F32)]
        + split(value, 3)
        + [jnp.zeros((13, width), F32)],
        axis=0,
    )
    return jnp.concatenate([high, high, low, tail], axis=0)


def value_column(rows):
    at = lax.broadcasted_iota(jnp.int32, (128, 128), 0)
    chosen = jnp.where((at >= 112) & (at < 115), 1.0, 0.0).astype(BF16)
    return jnp.dot(rows, chosen, preferred_element_type=F32)


def col_stack(pts, norm, rate):
    high, low = split(pts * (2.0 * LOG2E * rate), 2)
    one = jnp.ones_like(norm)
    width = pts.shape[1]
    tail = jnp.concatenate([one] * 3 + split(norm, 3) + [jnp.zeros((26, width), F32)], axis=0)
    return jnp.concatenate([high, low, high, tail], axis=0).astype(BF16)


def tile(rows, cols):
    return jnp.exp2(jnp.dot(rows, cols, preferred_element_type=F32))


def split_rows(row):
    return jnp.concatenate(
        split(row, 3) + [jnp.zeros((13, row.shape[1]), F32)], axis=0
    ).astype(BF16)


LEVELS = []
_first, _width = 0, LEAVES_DEV
while _width >= 2:
    LEVELS.append((_first, _width))
    _first, _width = _first + _width, _width // 2


def order_kernel(perm, rate_ref, pts, dirs, gt, rows_out, raw, held):
    rate = rate_ref[0]
    blocks = pts.shape[1] // 128

    def place(block, _):
        at = pl.multiple_of(block * 128, 128)
        part = pts[:, pl.ds(at, 128)]
        raw[pl.ds(at, 128), :] = row_stack(
            part, norm_row(part, rate), dirs[pl.ds(block, 1), :]
        ).T
        return 0

    lax.fori_loop(0, blocks, place, 0, unroll=4)

    def gather(group, _):
        base = pl.multiple_of(group * 32, 32)
        for i in range(32):
            held[pl.ds(base + i, 1), :] = raw[pl.ds(perm[base + i], 1), :]
        return 0

    lax.fori_loop(0, pts.shape[1] // 32, gather, 0)

    def leaf(j, _):
        at = pl.multiple_of(j * LEAF, LEAF)
        mine = held[pl.ds(at, LEAF), :]
        rows_out[j] = mine.astype(BF16)
        turned = mine.T
        gt[0:32, pl.ds(at, LEAF)] = turned[0:32] + turned[64:96]
        gt[32:40, pl.ds(at, LEAF)] = jnp.concatenate(
            [
                turned[112:113] + turned[113:114] + turned[114:115],
                turned[96:97] + turned[97:98] + turned[98:99],
                jnp.zeros((6, LEAF), F32),
            ],
            axis=0,
        )
        return 0

    lax.fori_loop(0, LEAVES_DEV, leaf, 0, unroll=4)


def down_kernel(
    tgt, src, cnt, first_ref, rate_ref, ridge_ref, perm, gt, left, right, rows, down,
    skel_hbm, image, cols, dirs, acc, turned_img, skel, skel_sem,
):
    rate = rate_ref[0]
    first = first_ref[0]
    fetch = pltpu.make_async_copy(skel_hbm.at[pl.ds(0, LEAVES_DEV)], skel, skel_sem)
    fetch.start()

    def load_cols(ref, base):
        def body(i, _):
            at = pl.multiple_of(i * LEAF, LEAF)
            cols[base + i] = col_stack(ref[0:32, pl.ds(at, LEAF)], ref[33:34, pl.ds(at, LEAF)], rate)
            dirs[base + i] = jnp.broadcast_to(ref[32:33, pl.ds(at, LEAF)], (8, LEAF))
            return 0

        lax.fori_loop(0, ref.shape[1] // LEAF, body, 0, unroll=2)

    load_cols(left, 0)
    load_cols(gt, REACH)
    load_cols(right, REACH + LEAVES_DEV)

    lane = lax.broadcasted_iota(jnp.int32, (LEAF, 128), 1)
    def far(j, _):
        node = skel[j]
        kern = tile(rows[j], col_stack(node, norm_row(node, rate), rate))
        kern = kern * down[pl.ds(j, 1), :]
        acc[0, j] = kern[:, 0:128] + kern[:, 128:256]
        for way in range(1, WAYS):
            acc[way, j] = jnp.zeros((LEAF, 128), F32)
        return 0

    fetch.wait()
    lax.fori_loop(0, LEAVES_DEV, far, 0, unroll=2)

    total = cnt[0]

    def near(step, _):
        for way in range(WAYS):
            slot = step * WAYS + way
            target = jnp.clip(tgt[slot] - first, 0, LEAVES_DEV - 1)
            source = jnp.clip(src[slot] - first + REACH, 0, LEAVES_DEV + 2 * REACH - 1)
            source = jnp.where(slot < total, source, target + REACH)
            weight = jnp.where(slot < total, dirs[source][0:1, :], 0.0)
            kern = tile(rows[target], cols[source]) * weight
            acc[way, target] += kern[:, 0:128] + kern[:, 128:256]
        return 0

    lax.fori_loop(0, (total + WAYS - 1) // WAYS, near, 0)

    turned_img[...] = jnp.zeros_like(turned_img)

    def gather_image(j, _):
        value = acc[0, j]
        for way in range(1, WAYS):
            value = value + acc[way, j]
        turned_img[...] = jnp.where(
            lane == j, jnp.sum(value, axis=1, keepdims=True), turned_img[...]
        )
        return 0

    lax.fori_loop(0, LEAVES_DEV, gather_image, 0)
    tree_image = turned_img[...].T

    grand = jnp.zeros((192, 128), F32)
    high_id = lax.broadcasted_iota(jnp.int32, (64, LEAF), 0)
    low_id = lax.broadcasted_iota(jnp.int32, (128, LEAF), 0)
    for j in range(LEAVES_DEV):
        at = perm[j : j + 1, :]
        value = tree_image[j : j + 1, :] + ridge_ref[0] * dirs[REACH + j][0:1, :]
        hot = high_id == (at >> 7)
        picked = jnp.concatenate(
            [jnp.where(hot, part, 0.0) for part in split(value, 3)], axis=0
        ).astype(BF16)
        low = jnp.where(low_id == (at & 127), 1.0, 0.0).astype(BF16)
        grand = grand + lax.dot_general(
            picked, low, (((1,), (1,)), ((), ())), preferred_element_type=F32
        )
    image[...] = grand[0:64] + grand[64:128] + grand[128:192]


PARAMS = pltpu.CompilerParams(vmem_limit_bytes=60 * 1024 * 1024)


def call_order(perm, rate, points, direction):
    count = points.shape[1]
    return pl.pallas_call(
        order_kernel,
        out_shape=(
            jax.ShapeDtypeStruct((40, count), F32),
            jax.ShapeDtypeStruct((LEAVES_DEV, LEAF, 128), BF16),
        ),
        in_specs=[SMEM, SMEM, VMEM, VMEM],
        out_specs=(VMEM, VMEM),
        scratch_shapes=[pltpu.VMEM((count, 128), F32), pltpu.VMEM((count, 128), F32)],
        compiler_params=PARAMS,
        name="tree_order",
    )(perm, rate, points, direction)


def call_down(tgt, src, cnt, first, rate, ridge, perm, gt, left, right, rows, down, skel):
    return pl.pallas_call(
        down_kernel,
        out_shape=jax.ShapeDtypeStruct((64, 128), F32),
        in_specs=[SMEM] * 6 + [VMEM] * 6 + [pl.BlockSpec(memory_space=pl.ANY)],
        out_specs=VMEM,
        scratch_shapes=[
            pltpu.VMEM((LEAVES_DEV + 2 * REACH, 128, LEAF), BF16),
            pltpu.VMEM((LEAVES_DEV + 2 * REACH, 8, LEAF), F32),
            pltpu.VMEM((WAYS, LEAVES_DEV, LEAF, 128), F32),
            pltpu.VMEM((LEAF, 128), F32),
            pltpu.VMEM((LEAVES_DEV, DIM, LEAF), F32),
            pltpu.SemaphoreType.DMA,
        ],
        compiler_params=PARAMS,
        name="near_far",
    )(tgt, src, cnt, first, rate, ridge, perm, gt, left, right, rows, down, skel)


def remote_params(collective_id):
    return pltpu.CompilerParams(
        vmem_limit_bytes=60 * 1024 * 1024, collective_id=collective_id, has_side_effects=True
    )


def signal(barrier, device):
    pl.semaphore_signal(
        barrier, inc=1, device_id={"leaf": device}, device_id_type=pl.DeviceIdType.MESH
    )


def remote(src, dst, send_sem, recv_sem, device):
    return pltpu.make_async_remote_copy(
        src_ref=src,
        dst_ref=dst,
        send_sem=send_sem,
        recv_sem=recv_sem,
        device_id={"leaf": device},
        device_id_type=pl.DeviceIdType.MESH,
    )


def cross_kernel(
    devices, rate_ref, rows, local_skel, skel, trans, local_hbm, gt, down_out, left, right,
    ups, coupled, local, columns, sent, slots, kerns, couple,
    halo_send, halo_recv, hop_send, hop_recv, local_sem,
):
    rate = rate_ref[0]
    me = lax.axis_index("leaf")
    levels = skel.shape[0]
    edge = left.shape[1]
    peers = []
    for level in range(levels):
        mask = 2**level
        peers.append(me + mask * (1 - 2 * ((me // mask) % 2)))
    has_left, has_right = me > 0, me < devices - 1

    fetch = pltpu.make_async_copy(local_hbm, local, local_sem)
    fetch.start()
    barrier = pltpu.get_barrier_semaphore()
    for peer in peers:
        signal(barrier, peer)
    for present, peer in ((has_left, me - 1), (has_right, me + 1)):

        @pl.when(present)
        def _():
            signal(barrier, peer)

    pl.semaphore_wait(
        barrier, levels + has_left.astype(jnp.int32) + has_right.astype(jnp.int32)
    )

    def hop(level):
        return remote(
            sent.at[level], slots.at[level], hop_send.at[level], hop_recv.at[level], peers[level]
        )

    to_left = remote(
        gt.at[:, pl.ds(0, edge)], right, halo_send.at[0], halo_recv.at[0], me - 1
    )
    to_right = remote(
        gt.at[:, pl.ds(gt.shape[1] - edge, edge)], left, halo_send.at[1], halo_recv.at[1], me + 1
    )

    pl.when(has_left)(to_left.start)
    pl.when(has_right)(to_right.start)

    def leaf(j, _):
        node = local_skel[j]
        mine = rows[j]
        kern = tile(mine, col_stack(node, norm_row(node, rate), rate))
        value = value_column(mine)
        ups[pl.ds(j, 1), :] = jnp.concatenate(
            [
                jnp.sum(kern[:, 0:128] * value, axis=0, keepdims=True),
                jnp.sum(kern[:, 128:256] * value, axis=0, keepdims=True),
            ],
            axis=1,
        )
        return 0

    lax.fori_loop(0, LEAVES_DEV, leaf, 0, unroll=4)
    fetch.wait()
    for first, width in LEVELS:
        for i in range(width // 2):
            total = jnp.zeros((16, LEAF), F32)
            for node in (first + 2 * i, first + 2 * i + 1):
                total = total + jnp.dot(
                    split_rows(ups[node : node + 1, :]), local[node], preferred_element_type=F32
                )
            ups[first + width + i : first + width + i + 1, :] = (
                jnp.sum(total, axis=0, keepdims=True) * half_root
            )

    current = ups[NODES : NODES + 1, :]
    sent[0] = jnp.broadcast_to(current, (8, LEAF))
    hop(0).start()

    lane = lax.broadcasted_iota(jnp.int32, (LEAF, 128), 1)
    columns[...] = jnp.zeros_like(columns)

    def pair(i, _):
        a, b = 2 * i, 2 * i + 1
        mine, other = local_skel[a], local_skel[b]
        up_a, up_b = ups[pl.ds(a, 1), :], ups[pl.ds(b, 1), :]
        mine_rows = row_stack(mine, norm_row(mine, rate), up_a).T.astype(BF16)
        kern = tile(mine_rows, col_stack(other, norm_row(other, rate), rate))
        value = value_column(mine_rows)
        coupled[pl.ds(b, 1), :] = jnp.concatenate(
            [
                jnp.sum(kern[:, 0:128] * value, axis=0, keepdims=True),
                jnp.sum(kern[:, 128:256] * value, axis=0, keepdims=True),
            ],
            axis=1,
        )
        columns[...] = jnp.where(
            lane == a, jnp.sum(kern * up_b, axis=1, keepdims=True), columns[...]
        )
        return 0

    def couplings(level, _):
        mine, other = skel[level, 0], skel[level, 1]
        norm = norm_row(mine, rate)
        kerns[level] = tile(
            row_stack(mine, norm, norm).T.astype(BF16),
            col_stack(other, norm_row(other, rate), rate),
        )
        return 0

    pairs = NODES // 2
    share = (pairs + levels - 1) // levels
    for level in range(levels):
        lax.fori_loop(
            min(share * level, pairs), min(share * (level + 1), pairs), pair, 0, unroll=2
        )
        if level == levels - 2:
            lax.fori_loop(0, levels, couplings, 0, unroll=2)
        hop(level).wait()
        if level < levels - 1:
            total = jnp.dot(
                split_rows(current), trans[level, 0], preferred_element_type=F32
            ) + jnp.dot(
                split_rows(slots[level][0:1]), trans[level, 1], preferred_element_type=F32
            )
            current = jnp.sum(total, axis=0, keepdims=True) * half_root
            sent[level + 1] = jnp.broadcast_to(current, (8, LEAF))
            hop(level + 1).start()
    picked = jnp.zeros((LEAF, 128), F32)
    for level in range(levels):
        value = jnp.sum(kerns[level] * slots[level][0:1], axis=1, keepdims=True)
        picked = jnp.where(lane == level, value, picked)
    couple[...] = picked.T
    current = couple[levels - 1 : levels, :]
    for level in range(levels - 2, -1, -1):
        moved = lax.dot_general(
            split_rows(current), trans[level, 0], (((1,), (1,)), ((), ())),
            preferred_element_type=F32,
        )
        current = couple[level : level + 1, :] + jnp.sum(moved, axis=0, keepdims=True)
    turned = columns[...].T
    down = {NODES: current}
    for level in range(len(LEVELS) - 1, -1, -1):
        start, width = LEVELS[level]
        for i in range(width // 2):
            parts = split_rows(down[start + width + i])
            for node in (start + 2 * i, start + 2 * i + 1):
                moved = lax.dot_general(
                    parts, local[node], (((1,), (1,)), ((), ())), preferred_element_type=F32
                )
                own = coupled[node : node + 1, :] if node % 2 else turned[node : node + 1]
                down[node] = own + jnp.sum(moved, axis=0, keepdims=True)
    for node in range(LEAVES_DEV):
        down_out[node : node + 1, :] = down[node]

    @pl.when(has_left)
    def _():
        to_left.wait_send()
        to_right.wait_recv()

    @pl.when(has_right)
    def _():
        to_right.wait_send()
        to_left.wait_recv()


def call_cross(devices, rate, rows, local_skel, skel, trans, local_trans, gt):
    levels = skel.shape[0]
    edge = REACH * LEAF
    far = pl.BlockSpec(memory_space=pl.ANY)
    return pl.pallas_call(
        functools.partial(cross_kernel, devices),
        out_shape=(
            jax.ShapeDtypeStruct((LEAVES_DEV, LEAF), F32),
            jax.ShapeDtypeStruct((40, edge), F32),
            jax.ShapeDtypeStruct((40, edge), F32),
        ),
        in_specs=[SMEM, VMEM, VMEM, VMEM, VMEM, far, far],
        out_specs=(VMEM, far, far),
        scratch_shapes=[
            pltpu.VMEM((64, LEAF), F32),
            pltpu.VMEM((64, LEAF), F32),
            pltpu.VMEM(local_trans.shape, BF16),
            pltpu.VMEM((LEAF, 128), F32),
            pltpu.VMEM((levels, 8, LEAF), F32),
            pltpu.VMEM((levels, 8, LEAF), F32),
            pltpu.VMEM((levels, LEAF, LEAF), F32),
            pltpu.VMEM((128, LEAF), F32),
            pltpu.SemaphoreType.DMA((2,)),
            pltpu.SemaphoreType.DMA((2,)),
            pltpu.SemaphoreType.DMA((levels,)),
            pltpu.SemaphoreType.DMA((levels,)),
            pltpu.SemaphoreType.DMA,
        ],
        compiler_params=remote_params(0),
        name="tree",
    )(rate, rows, local_skel, skel, trans, local_trans, gt)


def step_kernel(
    devices, image, residual, direction, factors, sent, slots, send_sem, recv_sem,
):
    me = lax.axis_index("leaf")
    barrier = pltpu.get_barrier_semaphore()

    def greet(offset, _):
        signal(barrier, (me + offset) % devices)
        return 0

    lax.fori_loop(1, devices, greet, 0)
    res, dire, img = residual[...], direction[...], image[...]
    sent[0] = jnp.concatenate(
        [
            jnp.sum(res * res, axis=0, keepdims=True),
            jnp.sum(dire * img, axis=0, keepdims=True),
            jnp.zeros((6, 128), F32),
        ],
        axis=0,
    )
    pl.semaphore_wait(barrier, devices - 1)

    def total(phase):
        def copy(offset):
            return remote(
                sent.at[phase],
                slots.at[phase, offset],
                send_sem.at[phase, offset],
                recv_sem.at[phase, offset],
                (me + offset) % devices,
            )

        def start(offset, _):
            copy(offset).start()
            return 0

        def finish(offset, running):
            copy(offset).wait()
            return running + slots[phase, offset]

        lax.fori_loop(1, devices, start, 0)
        lanes = lax.fori_loop(1, devices, finish, sent[phase])
        return jnp.sum(lanes, axis=1, keepdims=True)

    sums = total(0)
    norm_old = sums[0:1]
    step_size = norm_old / sums[1:2]
    new_res = res - step_size * img
    sent[1] = jnp.concatenate(
        [jnp.sum(new_res * new_res, axis=0, keepdims=True), jnp.zeros((7, 128), F32)], axis=0
    )
    norm_new = total(1)[0:1]
    factors[...] = jnp.concatenate(
        [
            jnp.broadcast_to(step_size, (8, 128)),
            jnp.broadcast_to(norm_new / (norm_old + epsilon), (8, 128)),
        ],
        axis=0,
    )


def update_kernel(
    factors, image, solution, residual, direction, new_solution, new_residual, new_direction
):
    step_size, turn = factors[0:1, :], factors[8:9, :]
    dire = direction[...]
    new_res = residual[...] - step_size * image[...]
    new_residual[...] = new_res
    new_solution[...] = solution[...] + step_size * dire
    new_direction[...] = new_res + turn * dire


def call_step(devices, image, solution, residual, direction):
    flat = jax.ShapeDtypeStruct((64, 128), F32)
    factors = pl.pallas_call(
        functools.partial(step_kernel, devices),
        out_shape=jax.ShapeDtypeStruct((16, 128), F32),
        in_specs=[VMEM] * 3,
        out_specs=VMEM,
        scratch_shapes=[
            pltpu.VMEM((2, 8, 128), F32),
            pltpu.VMEM((2, devices, 8, 128), F32),
            pltpu.SemaphoreType.DMA((2, devices)),
            pltpu.SemaphoreType.DMA((2, devices)),
        ],
        compiler_params=remote_params(1),
        name="step",
    )(image, residual, direction)
    return pl.pallas_call(
        update_kernel,
        out_shape=(flat, flat, flat),
        in_specs=[VMEM] * 5,
        out_specs=(VMEM,) * 3,
        name="update",
    )(factors, image, solution, residual, direction)


def shards(
    points,
    solution,
    residual,
    direction,
    ridge_weight,
    kernel_rate,
    tree_perm,
    local_skeleton,
    local_transfer,
    cross_skeleton,
    cross_transfer,
    near_target,
    near_source,
    tile_count,
):
    devices = lax.axis_size("leaf")
    folded = tuple(array.reshape(64, 128) for array in (solution, residual, direction))
    gt, rows = call_order(tree_perm[0], kernel_rate, points, folded[2])
    down, left, right = call_cross(
        devices, kernel_rate, rows, local_skeleton, cross_skeleton, cross_transfer,
        local_transfer, gt,
    )
    own_first = (lax.axis_index("leaf") * LEAVES_DEV).astype(jnp.int32).reshape(1)
    image = call_down(
        near_target, near_source, tile_count, own_first, kernel_rate, ridge_weight,
        tree_perm.reshape(LEAVES_DEV, LEAF), gt, left, right, rows, down, local_skeleton,
    )
    return tuple(array.reshape(-1) for array in call_step(devices, image, *folded))


def solution(mesh):
    return jax.shard_map(
        shards,
        mesh=mesh,
        in_specs=(
            P(None, ("groups", "leaf")),
            P(("groups", "leaf")),
            P(("groups", "leaf")),
            P(("groups", "leaf")),
            P("groups"),
            P("groups"),
            P(("groups", "leaf"), None),
            P(("groups", "leaf"), None, None),
            P(("groups", "leaf"), None, None),
            P(("groups", "leaf"), None, None, None),
            P(("groups", "leaf"), None, None, None),
            P(("groups", "leaf")),
            P(("groups", "leaf")),
            P(("groups", "leaf")),
        ),
        out_specs=(P(("groups", "leaf")), P(("groups", "leaf")), P(("groups", "leaf"))),
        check_vma=False,
    )
```

```python
import functools
import math

import jax
import jax.numpy as jnp
from jax import lax
from jax.experimental import pallas as pl
from jax.experimental.pallas import tpu as pltpu
from jax.sharding import PartitionSpec as P

LEAF = 256
LEAVES_DEV = 32
REACH = 16
DIM = 32
NODES = 62
WAYS = 8
SUMS = 2

epsilon = 1e-06
half_root = 0.5**0.5
LOG2E = math.log2(math.e)
F32 = jnp.float32
BF16 = jnp.bfloat16
VMEM = pl.BlockSpec(memory_space=pltpu.VMEM)
SMEM = pl.BlockSpec(memory_space=pltpu.SMEM)


def split(value, count):
    parts = []
    for _ in range(count):
        part = value.astype(BF16).astype(F32)
        parts.append(part)
        value = value - part
    return parts


def norm_row(pts, rate):
    return jnp.sum(pts * pts, axis=0, keepdims=True) * (-rate * LOG2E)


def row_stack(pts, norm, value):
    high, low = split(pts, 2)
    one = jnp.ones_like(norm)
    width = pts.shape[1]
    tail = jnp.concatenate(
        split(norm, 3)
        + [one] * 3
        + [jnp.zeros((10, width), F32)]
        + split(value, 3)
        + [jnp.zeros((13, width), F32)],
        axis=0,
    )
    return jnp.concatenate([high, high, low, tail], axis=0)


def value_column(rows):
    at = lax.broadcasted_iota(jnp.int32, (128, 128), 0)
    chosen = jnp.where((at >= 112) & (at < 115), 1.0, 0.0).astype(BF16)
    return jnp.dot(rows, chosen, preferred_element_type=F32)


def col_stack(pts, norm, rate):
    high, low = split(pts * (2.0 * LOG2E * rate), 2)
    one = jnp.ones_like(norm)
    width = pts.shape[1]
    tail = jnp.concatenate([one] * 3 + split(norm, 3) + [jnp.zeros((26, width), F32)], axis=0)
    return jnp.concatenate([high, low, high, tail], axis=0).astype(BF16)


def tile(rows, cols):
    return jnp.exp2(jnp.dot(rows, cols, preferred_element_type=F32))


def split_rows(row):
    return jnp.concatenate(
        split(row, 3) + [jnp.zeros((13, row.shape[1]), F32)], axis=0
    ).astype(BF16)


LEVELS = []
_first, _width = 0, LEAVES_DEV
while _width >= 2:
    LEVELS.append((_first, _width))
    _first, _width = _first + _width, _width // 2


def order_kernel(perm, rate_ref, pts, dirs, gt, dir_out, rows_out, raw, held):
    rate = rate_ref[0]
    blocks = pts.shape[1] // 128

    def place(block, _):
        at = pl.multiple_of(block * 128, 128)
        part = pts[:, pl.ds(at, 128)]
        raw[pl.ds(at, 128), :] = row_stack(
            part, norm_row(part, rate), dirs[pl.ds(block, 1), :]
        ).T
        return 0

    lax.fori_loop(0, blocks, place, 0, unroll=4)

    def gather(group, _):
        base = pl.multiple_of(group * 32, 32)
        for i in range(32):
            held[pl.ds(base + i, 1), :] = raw[pl.ds(perm[0, base + i], 1), :]
        return 0

    lax.fori_loop(0, pts.shape[1] // 32, gather, 0)

    to = lax.broadcasted_iota(jnp.int32, (48, 128), 0)
    of = lax.broadcasted_iota(jnp.int32, (48, 128), 1)
    point = (to < DIM) & ((of == to) | (of == to + 64))
    value = (to == DIM) & (of >= 112) & (of < 115)
    chosen = jnp.where(point | value, 1.0, 0.0).astype(BF16)

    def leaf(j, _):
        at = pl.multiple_of(j * LEAF, LEAF)
        mine = held[pl.ds(at, LEAF), :].astype(BF16)
        rows_out[j] = mine
        turned = lax.dot_general(
            chosen, mine, (((1,), (1,)), ((), ())), preferred_element_type=F32
        )
        gt[:, pl.ds(at, LEAF)] = turned[0:DIM]
        dir_out[pl.ds(j, 1), :] = turned[DIM : DIM + 1]
        return 0

    lax.fori_loop(0, LEAVES_DEV, leaf, 0, unroll=4)


def down_kernel(
    tgt, src, cnt, first_ref, rate_ref, ridge_ref, perm, gt, own_dir, left, left_dir,
    right, right_dir, rows, down, skel_hbm, image, cols, dirs, acc, turned_img, skel, skel_sem,
):
    rate = rate_ref[0]
    first = first_ref[0]
    fetch = pltpu.make_async_copy(skel_hbm.at[pl.ds(0, LEAVES_DEV)], skel, skel_sem)
    fetch.start()

    def load_cols(ref, dir_ref, base):
        def body(i, _):
            part = ref[:, pl.ds(pl.multiple_of(i * LEAF, LEAF), LEAF)]
            cols[base + i] = col_stack(part, norm_row(part, rate), rate)
            dirs[base + i] = jnp.broadcast_to(dir_ref[pl.ds(i, 1), :], (8, LEAF))
            return 0

        lax.fori_loop(0, ref.shape[1] // LEAF, body, 0, unroll=4)

    load_cols(left, left_dir, 0)
    load_cols(gt, own_dir, REACH)
    load_cols(right, right_dir, REACH + LEAVES_DEV)

    lane = lax.broadcasted_iota(jnp.int32, (LEAF, 128), 1)
    def far(j, _):
        node = skel[j]
        kern = tile(rows[j], col_stack(node, norm_row(node, rate), rate))
        kern = kern * down[pl.ds(j, 1), :]
        acc[0, j] = kern[:, 0:128] + kern[:, 128:256]
        for way in range(1, SUMS):
            acc[way, j] = jnp.zeros((LEAF, 128), F32)
        return 0

    fetch.wait()
    lax.fori_loop(0, LEAVES_DEV, far, 0, unroll=2)

    total = cnt[0]

    def near(step, _):
        for way in range(WAYS):
            slot = step * WAYS + way
            target = jnp.clip(tgt[slot] - first, 0, LEAVES_DEV - 1)
            source = jnp.clip(src[slot] - first + REACH, 0, LEAVES_DEV + 2 * REACH - 1)
            source = jnp.where(slot < total, source, target + REACH)
            weight = jnp.where(slot < total, dirs[source][0:1, :], 0.0)
            kern = tile(rows[target], cols[source]) * weight
            acc[way % SUMS, target] += kern[:, 0:128] + kern[:, 128:256]
        return 0

    lax.fori_loop(0, (total + WAYS - 1) // WAYS, near, 0)

    turned_img[...] = jnp.zeros_like(turned_img)

    def gather_image(j, _):
        value = acc[0, j]
        for way in range(1, SUMS):
            value = value + acc[way, j]
        turned_img[...] = jnp.where(
            lane == j, jnp.sum(value, axis=1, keepdims=True), turned_img[...]
        )
        return 0

    lax.fori_loop(0, LEAVES_DEV, gather_image, 0)
    tree_image = turned_img[...].T

    grand = jnp.zeros((192, 128), F32)
    high_id = lax.broadcasted_iota(jnp.int32, (64, LEAF), 0)
    low_id = lax.broadcasted_iota(jnp.int32, (128, LEAF), 0)
    for j in range(LEAVES_DEV):
        at = perm[j : j + 1, :]
        value = tree_image[j : j + 1, :] + ridge_ref[0] * dirs[REACH + j][0:1, :]
        hot = high_id == (at >> 7)
        picked = jnp.concatenate(
            [jnp.where(hot, part, 0.0) for part in split(value, 3)], axis=0
        ).astype(BF16)
        low = jnp.where(low_id == (at & 127), 1.0, 0.0).astype(BF16)
        grand = grand + lax.dot_general(
            picked, low, (((1,), (1,)), ((), ())), preferred_element_type=F32
        )
    image[...] = grand[0:64] + grand[64:128] + grand[128:192]


PARAMS = pltpu.CompilerParams(vmem_limit_bytes=60 * 1024 * 1024)


def call_order(perm, rate, points, direction):
    count = points.shape[1]
    return pl.pallas_call(
        order_kernel,
        out_shape=(
            jax.ShapeDtypeStruct((DIM, count), F32),
            jax.ShapeDtypeStruct((LEAVES_DEV, LEAF), F32),
            jax.ShapeDtypeStruct((LEAVES_DEV, LEAF, 128), BF16),
        ),
        in_specs=[SMEM, SMEM, VMEM, VMEM],
        out_specs=(VMEM, VMEM, VMEM),
        scratch_shapes=[pltpu.VMEM((count, 128), F32), pltpu.VMEM((count, 128), F32)],
        compiler_params=PARAMS,
        name="tree_order",
    )(perm, rate, points, direction)


def call_down(tgt, src, cnt, first, rate, ridge, perm, *arrays):
    return pl.pallas_call(
        down_kernel,
        out_shape=jax.ShapeDtypeStruct((64, 128), F32),
        in_specs=[SMEM] * 6 + [VMEM] * 9 + [pl.BlockSpec(memory_space=pl.ANY)],
        out_specs=VMEM,
        scratch_shapes=[
            pltpu.VMEM((LEAVES_DEV + 2 * REACH, 128, LEAF), BF16),
            pltpu.VMEM((LEAVES_DEV + 2 * REACH, 8, LEAF), F32),
            pltpu.VMEM((SUMS, LEAVES_DEV, LEAF, 128), F32),
            pltpu.VMEM((LEAF, 128), F32),
            pltpu.VMEM((LEAVES_DEV, DIM, LEAF), F32),
            pltpu.SemaphoreType.DMA,
        ],
        compiler_params=PARAMS,
        name="near_far",
    )(tgt, src, cnt, first, rate, ridge, perm, *arrays)


def remote_params(collective_id):
    return pltpu.CompilerParams(
        vmem_limit_bytes=60 * 1024 * 1024, collective_id=collective_id, has_side_effects=True
    )


def signal(barrier, device):
    pl.semaphore_signal(
        barrier, inc=1, device_id={"leaf": device}, device_id_type=pl.DeviceIdType.MESH
    )


def remote(src, dst, send_sem, recv_sem, device):
    return pltpu.make_async_remote_copy(
        src_ref=src,
        dst_ref=dst,
        send_sem=send_sem,
        recv_sem=recv_sem,
        device_id={"leaf": device},
        device_id_type=pl.DeviceIdType.MESH,
    )


def cross_kernel(
    devices, rate_ref, rows, local_skel, skel, trans, local_hbm, gt, own_dir,
    down_out, left, left_dir, right, right_dir,
    ups, coupled, local, columns, sent, slots, kerns, couple,
    halo_send, halo_recv, hop_send, hop_recv, local_sem,
):
    rate = rate_ref[0]
    me = lax.axis_index("leaf")
    levels = skel.shape[0]
    edge = left.shape[1]
    peers = []
    for level in range(levels):
        mask = 2**level
        peers.append(me + mask * (1 - 2 * ((me // mask) % 2)))
    has_left, has_right = me > 0, me < devices - 1

    fetch = pltpu.make_async_copy(local_hbm, local, local_sem)
    fetch.start()
    barrier = pltpu.get_barrier_semaphore()
    for peer in peers:
        signal(barrier, peer)
    for present, peer in ((has_left, me - 1), (has_right, me + 1)):

        @pl.when(present)
        def _():
            signal(barrier, peer)

    pl.semaphore_wait(
        barrier, levels + has_left.astype(jnp.int32) + has_right.astype(jnp.int32)
    )

    def hop(level):
        return remote(
            sent.at[level], slots.at[level], hop_send.at[level], hop_recv.at[level], peers[level]
        )

    to_left = (
        remote(gt.at[:, pl.ds(0, edge)], right, halo_send.at[0], halo_recv.at[0], me - 1),
        remote(own_dir.at[pl.ds(0, REACH)], right_dir, halo_send.at[1], halo_recv.at[1], me - 1),
    )
    to_right = (
        remote(
            gt.at[:, pl.ds(gt.shape[1] - edge, edge)], left, halo_send.at[2], halo_recv.at[2],
            me + 1,
        ),
        remote(
            own_dir.at[pl.ds(LEAVES_DEV - REACH, REACH)], left_dir, halo_send.at[3],
            halo_recv.at[3], me + 1,
        ),
    )

    @pl.when(has_left)
    def _():
        for copy in to_left:
            copy.start()

    @pl.when(has_right)
    def _():
        for copy in to_right:
            copy.start()

    def leaf(j, _):
        node = local_skel[j]
        mine = rows[j]
        kern = tile(mine, col_stack(node, norm_row(node, rate), rate))
        value = value_column(mine)
        ups[pl.ds(j, 1), :] = jnp.concatenate(
            [
                jnp.sum(kern[:, 0:128] * value, axis=0, keepdims=True),
                jnp.sum(kern[:, 128:256] * value, axis=0, keepdims=True),
            ],
            axis=1,
        )
        return 0

    lax.fori_loop(0, LEAVES_DEV, leaf, 0, unroll=4)
    fetch.wait()
    for first, width in LEVELS:
        for i in range(width // 2):
            total = jnp.zeros((16, LEAF), F32)
            for node in (first + 2 * i, first + 2 * i + 1):
                total = total + jnp.dot(
                    split_rows(ups[node : node + 1, :]), local[node], preferred_element_type=F32
                )
            ups[first + width + i : first + width + i + 1, :] = (
                jnp.sum(total, axis=0, keepdims=True) * half_root
            )

    current = ups[NODES : NODES + 1, :]
    sent[0] = jnp.broadcast_to(current, (8, LEAF))
    hop(0).start()

    lane = lax.broadcasted_iota(jnp.int32, (LEAF, 128), 1)
    columns[...] = jnp.zeros_like(columns)

    def pair(i, _):
        a, b = 2 * i, 2 * i + 1
        mine, other = local_skel[a], local_skel[b]
        up_a, up_b = ups[pl.ds(a, 1), :], ups[pl.ds(b, 1), :]
        mine_rows = row_stack(mine, norm_row(mine, rate), up_a).T.astype(BF16)
        kern = tile(mine_rows, col_stack(other, norm_row(other, rate), rate))
        value = value_column(mine_rows)
        coupled[pl.ds(b, 1), :] = jnp.concatenate(
            [
                jnp.sum(kern[:, 0:128] * value, axis=0, keepdims=True),
                jnp.sum(kern[:, 128:256] * value, axis=0, keepdims=True),
            ],
            axis=1,
        )
        columns[...] = jnp.where(
            lane == a, jnp.sum(kern * up_b, axis=1, keepdims=True), columns[...]
        )
        return 0

    def couplings(level, _):
        mine, other = skel[level, 0], skel[level, 1]
        norm = norm_row(mine, rate)
        kerns[level] = tile(
            row_stack(mine, norm, norm).T.astype(BF16),
            col_stack(other, norm_row(other, rate), rate),
        )
        return 0

    pairs = NODES // 2
    share = (pairs + levels - 1) // levels
    for level in range(levels):
        lax.fori_loop(
            min(share * level, pairs), min(share * (level + 1), pairs), pair, 0, unroll=2
        )
        if level == levels - 2:
            lax.fori_loop(0, levels, couplings, 0, unroll=2)
        hop(level).wait()
        if level < levels - 1:
            total = jnp.dot(
                split_rows(current), trans[level, 0], preferred_element_type=F32
            ) + jnp.dot(
                split_rows(slots[level][0:1]), trans[level, 1], preferred_element_type=F32
            )
            current = jnp.sum(total, axis=0, keepdims=True) * half_root
            sent[level + 1] = jnp.broadcast_to(current, (8, LEAF))
            hop(level + 1).start()
    picked = jnp.zeros((LEAF, 128), F32)
    for level in range(levels):
        value = jnp.sum(kerns[level] * slots[level][0:1], axis=1, keepdims=True)
        picked = jnp.where(lane == level, value, picked)
    couple[...] = picked.T
    current = couple[levels - 1 : levels, :]
    for level in range(levels - 2, -1, -1):
        moved = lax.dot_general(
            split_rows(current), trans[level, 0], (((1,), (1,)), ((), ())),
            preferred_element_type=F32,
        )
        current = couple[level : level + 1, :] + jnp.sum(moved, axis=0, keepdims=True)
    turned = columns[...].T
    down = {NODES: current}
    for level in range(len(LEVELS) - 1, -1, -1):
        start, width = LEVELS[level]
        for i in range(width // 2):
            parts = split_rows(down[start + width + i])
            for node in (start + 2 * i, start + 2 * i + 1):
                moved = lax.dot_general(
                    parts, local[node], (((1,), (1,)), ((), ())), preferred_element_type=F32
                )
                own = coupled[node : node + 1, :] if node % 2 else turned[node : node + 1]
                down[node] = own + jnp.sum(moved, axis=0, keepdims=True)
    for node in range(LEAVES_DEV):
        down_out[node : node + 1, :] = down[node]

    @pl.when(has_left)
    def _():
        for out, back in zip(to_left, to_right):
            out.wait_send()
            back.wait_recv()

    @pl.when(has_right)
    def _():
        for out, back in zip(to_right, to_left):
            out.wait_send()
            back.wait_recv()


def call_cross(devices, rate, rows, local_skel, skel, trans, local_trans, gt, own_dir):
    levels = skel.shape[0]
    edge = REACH * LEAF
    far = pl.BlockSpec(memory_space=pl.ANY)
    return pl.pallas_call(
        functools.partial(cross_kernel, devices),
        out_shape=(
            jax.ShapeDtypeStruct((LEAVES_DEV, LEAF), F32),
            jax.ShapeDtypeStruct((DIM, edge), F32),
            jax.ShapeDtypeStruct((REACH, LEAF), F32),
            jax.ShapeDtypeStruct((DIM, edge), F32),
            jax.ShapeDtypeStruct((REACH, LEAF), F32),
        ),
        in_specs=[SMEM, VMEM, VMEM, VMEM, VMEM, far, far, far],
        out_specs=(VMEM, far, far, far, far),
        scratch_shapes=[
            pltpu.VMEM((64, LEAF), F32),
            pltpu.VMEM((64, LEAF), F32),
            pltpu.VMEM(local_trans.shape, BF16),
            pltpu.VMEM((LEAF, 128), F32),
            pltpu.VMEM((levels, 8, LEAF), F32),
            pltpu.VMEM((levels, 8, LEAF), F32),
            pltpu.VMEM((levels, LEAF, LEAF), F32),
            pltpu.VMEM((128, LEAF), F32),
            pltpu.SemaphoreType.DMA((4,)),
            pltpu.SemaphoreType.DMA((4,)),
            pltpu.SemaphoreType.DMA((levels,)),
            pltpu.SemaphoreType.DMA((levels,)),
            pltpu.SemaphoreType.DMA,
        ],
        compiler_params=remote_params(0),
        name="tree",
    )(rate, rows, local_skel, skel, trans, local_trans, gt, own_dir)


def step_kernel(
    devices, image, residual, direction, factors, sent, slots, send_sem, recv_sem,
):
    me = lax.axis_index("leaf")
    barrier = pltpu.get_barrier_semaphore()

    def greet(offset, _):
        signal(barrier, (me + offset) % devices)
        return 0

    lax.fori_loop(1, devices, greet, 0)
    res, dire, img = residual[...], direction[...], image[...]
    sent[0] = jnp.concatenate(
        [
            jnp.sum(res * res, axis=0, keepdims=True),
            jnp.sum(dire * img, axis=0, keepdims=True),
            jnp.zeros((6, 128), F32),
        ],
        axis=0,
    )
    pl.semaphore_wait(barrier, devices - 1)

    def total(phase):
        def copy(offset):
            return remote(
                sent.at[phase],
                slots.at[phase, offset],
                send_sem.at[phase, offset],
                recv_sem.at[phase, offset],
                (me + offset) % devices,
            )

        def start(offset, _):
            copy(offset).start()
            return 0

        def finish(offset, running):
            copy(offset).wait()
            return running + slots[phase, offset]

        lax.fori_loop(1, devices, start, 0)
        lanes = lax.fori_loop(1, devices, finish, sent[phase])
        return jnp.sum(lanes, axis=1, keepdims=True)

    sums = total(0)
    norm_old = sums[0:1]
    step_size = norm_old / sums[1:2]
    new_res = res - step_size * img
    sent[1] = jnp.concatenate(
        [jnp.sum(new_res * new_res, axis=0, keepdims=True), jnp.zeros((7, 128), F32)], axis=0
    )
    norm_new = total(1)[0:1]
    factors[...] = jnp.concatenate(
        [
            jnp.broadcast_to(step_size, (8, 128)),
            jnp.broadcast_to(norm_new / (norm_old + epsilon), (8, 128)),
        ],
        axis=0,
    )


def update_kernel(
    factors, image, solution, residual, direction, new_solution, new_residual, new_direction
):
    step_size, turn = factors[0:1, :], factors[8:9, :]
    dire = direction[...]
    new_res = residual[...] - step_size * image[...]
    new_residual[...] = new_res
    new_solution[...] = solution[...] + step_size * dire
    new_direction[...] = new_res + turn * dire


def call_step(devices, image, solution, residual, direction):
    flat = jax.ShapeDtypeStruct((64, 128), F32)
    factors = pl.pallas_call(
        functools.partial(step_kernel, devices),
        out_shape=jax.ShapeDtypeStruct((16, 128), F32),
        in_specs=[VMEM] * 3,
        out_specs=VMEM,
        scratch_shapes=[
            pltpu.VMEM((2, 8, 128), F32),
            pltpu.VMEM((2, devices, 8, 128), F32),
            pltpu.SemaphoreType.DMA((2, devices)),
            pltpu.SemaphoreType.DMA((2, devices)),
        ],
        compiler_params=remote_params(1),
        name="step",
    )(image, residual, direction)
    return pl.pallas_call(
        update_kernel,
        out_shape=(flat, flat, flat),
        in_specs=[VMEM] * 5,
        out_specs=(VMEM,) * 3,
        name="update",
    )(factors, image, solution, residual, direction)


def shards(
    points,
    solution,
    residual,
    direction,
    ridge_weight,
    kernel_rate,
    tree_perm,
    local_skeleton,
    local_transfer,
    cross_skeleton,
    cross_transfer,
    near_target,
    near_source,
    tile_count,
):
    devices = lax.axis_size("leaf")
    folded = tuple(array.reshape(64, 128) for array in (solution, residual, direction))
    gt, own_dir, rows = call_order(tree_perm, kernel_rate, points, folded[2])
    down, left, left_dir, right, right_dir = call_cross(
        devices, kernel_rate, rows, local_skeleton, cross_skeleton, cross_transfer,
        local_transfer, gt, own_dir,
    )
    own_first = (lax.axis_index("leaf") * LEAVES_DEV).astype(jnp.int32).reshape(1)
    image = call_down(
        near_target, near_source, tile_count, own_first, kernel_rate, ridge_weight,
        tree_perm.reshape(LEAVES_DEV, LEAF), gt, own_dir, left, left_dir,
        right, right_dir, rows, down, local_skeleton,
    )
    return tuple(array.reshape(-1) for array in call_step(devices, image, *folded))


def solution(mesh):
    return jax.shard_map(
        shards,
        mesh=mesh,
        in_specs=(
            P(None, ("groups", "leaf")),
            P(("groups", "leaf")),
            P(("groups", "leaf")),
            P(("groups", "leaf")),
            P("groups"),
            P("groups"),
            P(("groups", "leaf"), None),
            P(("groups", "leaf"), None, None),
            P(("groups", "leaf"), None, None),
            P(("groups", "leaf"), None, None, None),
            P(("groups", "leaf"), None, None, None),
            P(("groups", "leaf")),
            P(("groups", "leaf")),
            P(("groups", "leaf")),
        ),
        out_specs=(P(("groups", "leaf")), P(("groups", "leaf")), P(("groups", "leaf"))),
        check_vma=False,
    )
```

```python
import functools
import math

import jax
import jax.numpy as jnp
from jax import lax
from jax.experimental import pallas as pl
from jax.experimental.pallas import tpu as pltpu
from jax.sharding import PartitionSpec as P

LEAF = 256
LEAVES_DEV = 32
REACH = 16
DIM = 32
NODES = 62
WAYS = 16
SUMS = 2

epsilon = 1e-06
half_root = 0.5**0.5
LOG2E = math.log2(math.e)
F32 = jnp.float32
BF16 = jnp.bfloat16
VMEM = pl.BlockSpec(memory_space=pltpu.VMEM)
SMEM = pl.BlockSpec(memory_space=pltpu.SMEM)


def split(value, count):
    parts = []
    for _ in range(count):
        part = value.astype(BF16).astype(F32)
        parts.append(part)
        value = value - part
    return parts


def norm_row(pts, rate):
    return jnp.sum(pts * pts, axis=0, keepdims=True) * (-rate * LOG2E)


def row_stack(pts, norm, value):
    high, low = split(pts, 2)
    one = jnp.ones_like(norm)
    width = pts.shape[1]
    tail = jnp.concatenate(
        split(norm, 3)
        + [one] * 3
        + [jnp.zeros((10, width), F32)]
        + split(value, 3)
        + [jnp.zeros((13, width), F32)],
        axis=0,
    )
    return jnp.concatenate([high, high, low, tail], axis=0)


def value_column(rows):
    at = lax.broadcasted_iota(jnp.int32, (128, 128), 0)
    chosen = jnp.where((at >= 112) & (at < 115), 1.0, 0.0).astype(BF16)
    return jnp.dot(rows, chosen, preferred_element_type=F32)


def col_stack(pts, norm, rate):
    high, low = split(pts * (2.0 * LOG2E * rate), 2)
    one = jnp.ones_like(norm)
    width = pts.shape[1]
    tail = jnp.concatenate([one] * 3 + split(norm, 3) + [jnp.zeros((26, width), F32)], axis=0)
    return jnp.concatenate([high, low, high, tail], axis=0).astype(BF16)


def tile(rows, cols):
    return jnp.exp2(jnp.dot(rows, cols, preferred_element_type=F32))


def split_rows(row):
    return jnp.concatenate(
        split(row, 3) + [jnp.zeros((13, row.shape[1]), F32)], axis=0
    ).astype(BF16)


LEVELS = []
_first, _width = 0, LEAVES_DEV
while _width >= 2:
    LEVELS.append((_first, _width))
    _first, _width = _first + _width, _width // 2


def order_kernel(perm, rate_ref, pts, dirs, gt, dir_out, rows_out, raw, held):
    rate = rate_ref[0]
    blocks = pts.shape[1] // 128

    def place(block, _):
        at = pl.multiple_of(block * 128, 128)
        part = pts[:, pl.ds(at, 128)]
        raw[pl.ds(at, 128), :] = row_stack(
            part, norm_row(part, rate), dirs[pl.ds(block, 1), :]
        ).T
        return 0

    lax.fori_loop(0, blocks, place, 0, unroll=4)

    def gather(group, _):
        base = pl.multiple_of(group * 32, 32)
        for i in range(32):
            held[pl.ds(base + i, 1), :] = raw[pl.ds(perm[0, base + i], 1), :]
        return 0

    lax.fori_loop(0, pts.shape[1] // 32, gather, 0)

    to = lax.broadcasted_iota(jnp.int32, (48, 128), 0)
    of = lax.broadcasted_iota(jnp.int32, (48, 128), 1)
    point = (to < DIM) & ((of == to) | (of == to + 64))
    value = (to == DIM) & (of >= 112) & (of < 115)
    chosen = jnp.where(point | value, 1.0, 0.0).astype(BF16)

    def leaf(j, _):
        at = pl.multiple_of(j * LEAF, LEAF)
        mine = held[pl.ds(at, LEAF), :].astype(BF16)
        rows_out[j] = mine
        turned = lax.dot_general(
            chosen, mine, (((1,), (1,)), ((), ())), preferred_element_type=F32
        )
        gt[:, pl.ds(at, LEAF)] = turned[0:DIM]
        dir_out[pl.ds(j, 1), :] = turned[DIM : DIM + 1]
        return 0

    lax.fori_loop(0, LEAVES_DEV, leaf, 0, unroll=4)


def down_kernel(
    tgt, src, cnt, first_ref, rate_ref, ridge_ref, perm, gt, own_dir, left, left_dir,
    right, right_dir, rows, down, skel_hbm, image, cols, dirs, acc, turned_img, skel, skel_sem,
):
    rate = rate_ref[0]
    first = first_ref[0]
    fetch = pltpu.make_async_copy(skel_hbm.at[pl.ds(0, LEAVES_DEV)], skel, skel_sem)
    fetch.start()

    def load_cols(ref, dir_ref, base):
        def body(i, _):
            part = ref[:, pl.ds(pl.multiple_of(i * LEAF, LEAF), LEAF)]
            cols[base + i] = col_stack(part, norm_row(part, rate), rate)
            dirs[base + i] = jnp.broadcast_to(dir_ref[pl.ds(i, 1), :], (8, LEAF))
            return 0

        lax.fori_loop(0, ref.shape[1] // LEAF, body, 0, unroll=4)

    load_cols(left, left_dir, 0)
    load_cols(gt, own_dir, REACH)
    load_cols(right, right_dir, REACH + LEAVES_DEV)

    lane = lax.broadcasted_iota(jnp.int32, (LEAF, 128), 1)
    def far(j, _):
        node = skel[j]
        kern = tile(rows[j], col_stack(node, norm_row(node, rate), rate))
        kern = kern * down[pl.ds(j, 1), :]
        acc[0, j] = kern[:, 0:128] + kern[:, 128:256]
        for way in range(1, SUMS):
            acc[way, j] = jnp.zeros((LEAF, 128), F32)
        return 0

    fetch.wait()
    lax.fori_loop(0, LEAVES_DEV, far, 0, unroll=4)

    total = cnt[0]

    def near(step, _):
        for way in range(WAYS):
            slot = step * WAYS + way
            target = jnp.clip(tgt[slot] - first, 0, LEAVES_DEV - 1)
            source = jnp.clip(src[slot] - first + REACH, 0, LEAVES_DEV + 2 * REACH - 1)
            source = jnp.where(slot < total, source, target + REACH)
            weight = jnp.where(slot < total, dirs[source][0:1, :], 0.0)
            kern = tile(rows[target], cols[source]) * weight
            acc[way % SUMS, target] += kern[:, 0:128] + kern[:, 128:256]
        return 0

    lax.fori_loop(0, (total + WAYS - 1) // WAYS, near, 0)

    turned_img[...] = jnp.zeros_like(turned_img)

    def gather_image(j, _):
        value = acc[0, j]
        for way in range(1, SUMS):
            value = value + acc[way, j]
        turned_img[...] = jnp.where(
            lane == j, jnp.sum(value, axis=1, keepdims=True), turned_img[...]
        )
        return 0

    lax.fori_loop(0, LEAVES_DEV, gather_image, 0, unroll=2)
    tree_image = turned_img[...].T

    grand = jnp.zeros((192, 128), F32)
    high_id = lax.broadcasted_iota(jnp.int32, (64, LEAF), 0)
    low_id = lax.broadcasted_iota(jnp.int32, (128, LEAF), 0)
    for j in range(LEAVES_DEV):
        at = perm[:, j * LEAF : (j + 1) * LEAF]
        value = tree_image[j : j + 1, :] + ridge_ref[0] * dirs[REACH + j][0:1, :]
        hot = high_id == (at >> 7)
        picked = jnp.concatenate(
            [jnp.where(hot, part, 0.0) for part in split(value, 3)], axis=0
        ).astype(BF16)
        low = jnp.where(low_id == (at & 127), 1.0, 0.0).astype(BF16)
        grand = grand + lax.dot_general(
            picked, low, (((1,), (1,)), ((), ())), preferred_element_type=F32
        )
    image[...] = grand[0:64] + grand[64:128] + grand[128:192]


PARAMS = pltpu.CompilerParams(vmem_limit_bytes=60 * 1024 * 1024)


def call_order(perm, rate, points, direction):
    count = points.shape[1]
    return pl.pallas_call(
        order_kernel,
        out_shape=(
            jax.ShapeDtypeStruct((DIM, count), F32),
            jax.ShapeDtypeStruct((LEAVES_DEV, LEAF), F32),
            jax.ShapeDtypeStruct((LEAVES_DEV, LEAF, 128), BF16),
        ),
        in_specs=[SMEM, SMEM, VMEM, VMEM],
        out_specs=(VMEM, VMEM, VMEM),
        scratch_shapes=[pltpu.VMEM((count, 128), F32), pltpu.VMEM((count, 128), F32)],
        compiler_params=PARAMS,
        name="tree_order",
    )(perm, rate, points, direction)


def call_down(tgt, src, cnt, first, rate, ridge, perm, *arrays):
    return pl.pallas_call(
        down_kernel,
        out_shape=jax.ShapeDtypeStruct((64, 128), F32),
        in_specs=[SMEM] * 6 + [VMEM] * 9 + [pl.BlockSpec(memory_space=pl.ANY)],
        out_specs=VMEM,
        scratch_shapes=[
            pltpu.VMEM((LEAVES_DEV + 2 * REACH, 128, LEAF), BF16),
            pltpu.VMEM((LEAVES_DEV + 2 * REACH, 8, LEAF), F32),
            pltpu.VMEM((SUMS, LEAVES_DEV, LEAF, 128), F32),
            pltpu.VMEM((LEAF, 128), F32),
            pltpu.VMEM((LEAVES_DEV, DIM, LEAF), F32),
            pltpu.SemaphoreType.DMA,
        ],
        compiler_params=PARAMS,
        name="near_far",
    )(tgt, src, cnt, first, rate, ridge, perm, *arrays)


def remote_params(collective_id):
    return pltpu.CompilerParams(
        vmem_limit_bytes=60 * 1024 * 1024, collective_id=collective_id, has_side_effects=True
    )


def signal(barrier, device):
    pl.semaphore_signal(
        barrier, inc=1, device_id={"leaf": device}, device_id_type=pl.DeviceIdType.MESH
    )


def remote(src, dst, send_sem, recv_sem, device):
    return pltpu.make_async_remote_copy(
        src_ref=src,
        dst_ref=dst,
        send_sem=send_sem,
        recv_sem=recv_sem,
        device_id={"leaf": device},
        device_id_type=pl.DeviceIdType.MESH,
    )


def cross_kernel(
    devices, rate_ref, rows, local_skel, skel, trans, local_hbm, gt, own_dir,
    down_out, left, left_dir, right, right_dir,
    ups, coupled, local, columns, sent, slots, kerns, couple,
    halo_send, halo_recv, hop_send, hop_recv, local_sem,
):
    rate = rate_ref[0]
    me = lax.axis_index("leaf")
    levels = skel.shape[0]
    edge = left.shape[1]
    peers = []
    for level in range(levels):
        mask = 2**level
        peers.append(me + mask * (1 - 2 * ((me // mask) % 2)))
    has_left, has_right = me > 0, me < devices - 1

    fetch = pltpu.make_async_copy(local_hbm, local, local_sem)
    fetch.start()
    barrier = pltpu.get_barrier_semaphore()
    for peer in peers:
        signal(barrier, peer)
    for present, peer in ((has_left, me - 1), (has_right, me + 1)):

        @pl.when(present)
        def _():
            signal(barrier, peer)

    pl.semaphore_wait(
        barrier, levels + has_left.astype(jnp.int32) + has_right.astype(jnp.int32)
    )

    def hop(level):
        return remote(
            sent.at[level], slots.at[level], hop_send.at[level], hop_recv.at[level], peers[level]
        )

    to_left = (
        remote(gt.at[:, pl.ds(0, edge)], right, halo_send.at[0], halo_recv.at[0], me - 1),
        remote(own_dir.at[pl.ds(0, REACH)], right_dir, halo_send.at[1], halo_recv.at[1], me - 1),
    )
    to_right = (
        remote(
            gt.at[:, pl.ds(gt.shape[1] - edge, edge)], left, halo_send.at[2], halo_recv.at[2],
            me + 1,
        ),
        remote(
            own_dir.at[pl.ds(LEAVES_DEV - REACH, REACH)], left_dir, halo_send.at[3],
            halo_recv.at[3], me + 1,
        ),
    )

    @pl.when(has_left)
    def _():
        for copy in to_left:
            copy.start()

    @pl.when(has_right)
    def _():
        for copy in to_right:
            copy.start()

    def leaf(j, _):
        node = local_skel[j]
        mine = rows[j]
        kern = tile(mine, col_stack(node, norm_row(node, rate), rate))
        value = value_column(mine)
        ups[pl.ds(j, 1), :] = jnp.concatenate(
            [
                jnp.sum(kern[:, 0:128] * value, axis=0, keepdims=True),
                jnp.sum(kern[:, 128:256] * value, axis=0, keepdims=True),
            ],
            axis=1,
        )
        return 0

    lax.fori_loop(0, LEAVES_DEV, leaf, 0, unroll=4)
    fetch.wait()
    for first, width in LEVELS:
        for i in range(width // 2):
            total = jnp.zeros((16, LEAF), F32)
            for node in (first + 2 * i, first + 2 * i + 1):
                total = total + jnp.dot(
                    split_rows(ups[node : node + 1, :]), local[node], preferred_element_type=F32
                )
            ups[first + width + i : first + width + i + 1, :] = (
                jnp.sum(total, axis=0, keepdims=True) * half_root
            )

    current = ups[NODES : NODES + 1, :]
    sent[0] = jnp.broadcast_to(current, (8, LEAF))
    hop(0).start()

    lane = lax.broadcasted_iota(jnp.int32, (LEAF, 128), 1)
    columns[...] = jnp.zeros_like(columns)

    def pair(i, _):
        a, b = 2 * i, 2 * i + 1
        mine, other = local_skel[a], local_skel[b]
        up_a, up_b = ups[pl.ds(a, 1), :], ups[pl.ds(b, 1), :]
        mine_rows = row_stack(mine, norm_row(mine, rate), up_a).T.astype(BF16)
        kern = tile(mine_rows, col_stack(other, norm_row(other, rate), rate))
        value = value_column(mine_rows)
        coupled[pl.ds(b, 1), :] = jnp.concatenate(
            [
                jnp.sum(kern[:, 0:128] * value, axis=0, keepdims=True),
                jnp.sum(kern[:, 128:256] * value, axis=0, keepdims=True),
            ],
            axis=1,
        )
        columns[...] = jnp.where(
            lane == a, jnp.sum(kern * up_b, axis=1, keepdims=True), columns[...]
        )
        return 0

    def couplings(level, _):
        mine, other = skel[level, 0], skel[level, 1]
        norm = norm_row(mine, rate)
        kerns[level] = tile(
            row_stack(mine, norm, norm).T.astype(BF16),
            col_stack(other, norm_row(other, rate), rate),
        )
        return 0

    pairs = NODES // 2
    share = (pairs + levels - 1) // levels
    for level in range(levels):
        lax.fori_loop(
            min(share * level, pairs), min(share * (level + 1), pairs), pair, 0, unroll=2
        )
        if level == levels - 2:
            lax.fori_loop(0, levels, couplings, 0, unroll=2)
        hop(level).wait()
        if level < levels - 1:
            total = jnp.dot(
                split_rows(current), trans[level, 0], preferred_element_type=F32
            ) + jnp.dot(
                split_rows(slots[level][0:1]), trans[level, 1], preferred_element_type=F32
            )
            current = jnp.sum(total, axis=0, keepdims=True) * half_root
            sent[level + 1] = jnp.broadcast_to(current, (8, LEAF))
            hop(level + 1).start()
    picked = jnp.zeros((LEAF, 128), F32)
    for level in range(levels):
        value = jnp.sum(kerns[level] * slots[level][0:1], axis=1, keepdims=True)
        picked = jnp.where(lane == level, value, picked)
    couple[...] = picked.T
    current = couple[levels - 1 : levels, :]
    for level in range(levels - 2, -1, -1):
        moved = lax.dot_general(
            split_rows(current), trans[level, 0], (((1,), (1,)), ((), ())),
            preferred_element_type=F32,
        )
        current = couple[level : level + 1, :] + jnp.sum(moved, axis=0, keepdims=True)
    turned = columns[...].T
    down = {NODES: current}
    for level in range(len(LEVELS) - 1, -1, -1):
        start, width = LEVELS[level]
        for i in range(width // 2):
            parts = split_rows(down[start + width + i])
            for node in (start + 2 * i, start + 2 * i + 1):
                moved = lax.dot_general(
                    parts, local[node], (((1,), (1,)), ((), ())), preferred_element_type=F32
                )
                own = coupled[node : node + 1, :] if node % 2 else turned[node : node + 1]
                down[node] = own + jnp.sum(moved, axis=0, keepdims=True)
    for node in range(LEAVES_DEV):
        down_out[node : node + 1, :] = down[node]

    @pl.when(has_left)
    def _():
        for out, back in zip(to_left, to_right):
            out.wait_send()
            back.wait_recv()

    @pl.when(has_right)
    def _():
        for out, back in zip(to_right, to_left):
            out.wait_send()
            back.wait_recv()


def call_cross(devices, rate, rows, local_skel, skel, trans, local_trans, gt, own_dir):
    levels = skel.shape[0]
    edge = REACH * LEAF
    far = pl.BlockSpec(memory_space=pl.ANY)
    return pl.pallas_call(
        functools.partial(cross_kernel, devices),
        out_shape=(
            jax.ShapeDtypeStruct((LEAVES_DEV, LEAF), F32),
            jax.ShapeDtypeStruct((DIM, edge), F32),
            jax.ShapeDtypeStruct((REACH, LEAF), F32),
            jax.ShapeDtypeStruct((DIM, edge), F32),
            jax.ShapeDtypeStruct((REACH, LEAF), F32),
        ),
        in_specs=[SMEM, VMEM, VMEM, VMEM, VMEM, far, far, far],
        out_specs=(VMEM, far, far, far, far),
        scratch_shapes=[
            pltpu.VMEM((64, LEAF), F32),
            pltpu.VMEM((64, LEAF), F32),
            pltpu.VMEM(local_trans.shape, BF16),
            pltpu.VMEM((LEAF, 128), F32),
            pltpu.VMEM((levels, 8, LEAF), F32),
            pltpu.VMEM((levels, 8, LEAF), F32),
            pltpu.VMEM((levels, LEAF, LEAF), F32),
            pltpu.VMEM((128, LEAF), F32),
            pltpu.SemaphoreType.DMA((4,)),
            pltpu.SemaphoreType.DMA((4,)),
            pltpu.SemaphoreType.DMA((levels,)),
            pltpu.SemaphoreType.DMA((levels,)),
            pltpu.SemaphoreType.DMA,
        ],
        compiler_params=remote_params(0),
        name="tree",
    )(rate, rows, local_skel, skel, trans, local_trans, gt, own_dir)


def step_kernel(
    devices, image, residual, direction, factors, sent, slots, send_sem, recv_sem,
):
    me = lax.axis_index("leaf")
    barrier = pltpu.get_barrier_semaphore()

    def greet(offset, _):
        signal(barrier, (me + offset) % devices)
        return 0

    lax.fori_loop(1, devices, greet, 0)
    res, dire, img = residual[...], direction[...], image[...]
    sent[0] = jnp.concatenate(
        [
            jnp.sum(res * res, axis=0, keepdims=True),
            jnp.sum(dire * img, axis=0, keepdims=True),
            jnp.zeros((6, 128), F32),
        ],
        axis=0,
    )
    pl.semaphore_wait(barrier, devices - 1)

    def total(phase):
        def copy(offset):
            return remote(
                sent.at[phase],
                slots.at[phase, offset],
                send_sem.at[phase, offset],
                recv_sem.at[phase, offset],
                (me + offset) % devices,
            )

        def start(offset, _):
            copy(offset).start()
            return 0

        def finish(offset, running):
            copy(offset).wait()
            return running + slots[phase, offset]

        lax.fori_loop(1, devices, start, 0)
        lanes = lax.fori_loop(1, devices, finish, sent[phase])
        return jnp.sum(lanes, axis=1, keepdims=True)

    sums = total(0)
    norm_old = sums[0:1]
    step_size = norm_old / sums[1:2]
    new_res = res - step_size * img
    sent[1] = jnp.concatenate(
        [jnp.sum(new_res * new_res, axis=0, keepdims=True), jnp.zeros((7, 128), F32)], axis=0
    )
    norm_new = total(1)[0:1]
    factors[...] = jnp.concatenate(
        [
            jnp.broadcast_to(step_size, (8, 128)),
            jnp.broadcast_to(norm_new / (norm_old + epsilon), (8, 128)),
        ],
        axis=0,
    )


def update_kernel(
    factors, image, solution, residual, direction, new_solution, new_residual, new_direction
):
    step_size, turn = factors[0:1, :], factors[8:9, :]
    dire = direction[...]
    new_res = residual[...] - step_size * image[...]
    new_residual[...] = new_res
    new_solution[...] = solution[...] + step_size * dire
    new_direction[...] = new_res + turn * dire


def call_step(devices, image, solution, residual, direction):
    flat = jax.ShapeDtypeStruct((64, 128), F32)
    factors = pl.pallas_call(
        functools.partial(step_kernel, devices),
        out_shape=jax.ShapeDtypeStruct((16, 128), F32),
        in_specs=[VMEM] * 3,
        out_specs=VMEM,
        scratch_shapes=[
            pltpu.VMEM((2, 8, 128), F32),
            pltpu.VMEM((2, devices, 8, 128), F32),
            pltpu.SemaphoreType.DMA((2, devices)),
            pltpu.SemaphoreType.DMA((2, devices)),
        ],
        compiler_params=remote_params(1),
        name="step",
    )(image, residual, direction)
    return pl.pallas_call(
        update_kernel,
        out_shape=(flat, flat, flat),
        in_specs=[VMEM] * 5,
        out_specs=(VMEM,) * 3,
        name="update",
    )(factors, image, solution, residual, direction)


def shards(
    points,
    solution,
    residual,
    direction,
    ridge_weight,
    kernel_rate,
    tree_perm,
    local_skeleton,
    local_transfer,
    cross_skeleton,
    cross_transfer,
    near_target,
    near_source,
    tile_count,
):
    devices = lax.axis_size("leaf")
    folded = tuple(array.reshape(64, 128) for array in (solution, residual, direction))
    gt, own_dir, rows = call_order(tree_perm, kernel_rate, points, folded[2])
    down, left, left_dir, right, right_dir = call_cross(
        devices, kernel_rate, rows, local_skeleton, cross_skeleton, cross_transfer,
        local_transfer, gt, own_dir,
    )
    own_first = (lax.axis_index("leaf") * LEAVES_DEV).astype(jnp.int32).reshape(1)
    image = call_down(
        near_target, near_source, tile_count, own_first, kernel_rate, ridge_weight,
        tree_perm, gt, own_dir, left, left_dir,
        right, right_dir, rows, down, local_skeleton,
    )
    return tuple(array.reshape(-1) for array in call_step(devices, image, *folded))


def solution(mesh):
    return jax.shard_map(
        shards,
        mesh=mesh,
        in_specs=(
            P(None, ("groups", "leaf")),
            P(("groups", "leaf")),
            P(("groups", "leaf")),
            P(("groups", "leaf")),
            P("groups"),
            P("groups"),
            P(("groups", "leaf"), None),
            P(("groups", "leaf"), None, None),
            P(("groups", "leaf"), None, None),
            P(("groups", "leaf"), None, None, None),
            P(("groups", "leaf"), None, None, None),
            P(("groups", "leaf")),
            P(("groups", "leaf")),
            P(("groups", "leaf")),
        ),
        out_specs=(P(("groups", "leaf")), P(("groups", "leaf")), P(("groups", "leaf"))),
        check_vma=False,
    )
```
